256 devices in a mesh: grp: 8 (over x, z_lo), dev: 32 (over z_hi, y, core).
Axes of the slice: x: 4, y: 4, z: 8 (z_hi: 4, z_lo: 2; z = z_hi * 2 + z_lo), core: 2. Of those that a mesh axis runs over, the one named last changes fastest.
Arguments:
- image_emb: float32 [32768, 1152], P(('grp', 'dev')), may hold values from -0.18 to 0.18
- text_emb: float32 [32768, 1152], P(('grp', 'dev')), may hold values from -0.18 to 0.18
- temp: float32 [], replicated, may hold values from 6 to 12
- bias: float32 [], replicated, may hold values from -4 to -2
Outputs:
- grad_image: float32 [32768, 1152], P(('grp', 'dev'))
- grad_text: float32 [32768, 1152], P(('grp', 'dev'))
The draws below stay inside these ranges and needn't reach their ends.
All inputs are finite; a program needn't handle non-finite values.
Results may differ from the reference program's by a relative error of at most 0.0053.
Values may be sent and summed in bfloat16 or wider, within the bound.
No kernel may reach another device: no remote copies, remote signals or barrier semaphores. Data moves between devices by JAX's collectives and lax.ppermute only.
A program may use at most 128 MiB of HBM per device.

```python
import jax
import jax.numpy as jnp
from jax import lax

D = 1152
ROWS_DEV = 128
STEPS = 3
BATCH = 32768
N_GRP = 8
N_DEV = 32


def level_of(key, shape, shards, low, high):
    loudness = 1.0
    for dim, blocks in shards:
        heights = jax.random.uniform(jax.random.fold_in(jax.random.fold_in(key, 6), dim), (blocks,), jnp.float32, low / len(shards), high / len(shards))
        loudness = loudness * jnp.repeat(jnp.exp(heights), shape[dim] // blocks).reshape((-1,) + (1,) * (len(shape) - 1 - dim))
    return loudness


def scatter_about(own_key, shape, spread, bound, split=(), kind=jnp.bfloat16):
    entries = spread * jax.random.normal(own_key, shape, jnp.float32)
    if split:
        entries = entries * level_of(own_key, shape, split, -0.22, 0.18)
    return jnp.clip(entries, -bound, bound).astype(kind)


def setup_inputs(seed: int = 0) -> dict:
    arg_keys = jax.random.split(jax.random.key(seed), 5)
    return {
        "image_emb": scatter_about(arg_keys[0], (BATCH, D), 0.03, 0.18, ((0, 256),), jnp.float32),
        "text_emb": scatter_about(arg_keys[1], (BATCH, D), 0.03, 0.18, ((0, 256),), jnp.float32),
        "temp": jnp.clip(jax.random.uniform(arg_keys[2], (), jnp.float32, 6.0, 12.0), 6.0, 12.0),
        "bias": jnp.clip(jax.random.uniform(arg_keys[3], (), jnp.float32, -4.0, -2.0), -4.0, -2.0),
    }


def unit_rows(values):
    inverse = lax.rsqrt(lax.optimization_barrier(jnp.sum(values * values, axis=1, keepdims=True)) + 1e-06)
    return (values * inverse, inverse)

def back_rows(unit, inverse, upstream):
    return inverse * (upstream - unit * lax.optimization_barrier(jnp.sum(unit * upstream, axis=1, keepdims=True)))

def reference(image_emb, text_emb, temp, bias):
    group_rows = ROWS_DEV * N_DEV
    img_unit, img_inv = unit_rows(image_emb)
    txt_unit, txt_inv = unit_rows(text_emb)
    img_low = img_unit.astype(jnp.bfloat16)
    txt_low = txt_unit.astype(jnp.bfloat16)
    grad_u = [jnp.zeros((group_rows, D), jnp.float32) for group in range(N_GRP)]
    grad_v = [jnp.zeros((group_rows, D), jnp.float32) for group in range(N_GRP)]
    ident = (jnp.arange(group_rows)[:, None] == jnp.arange(group_rows)[None, :]).astype(jnp.float32)
    for group in range(N_GRP):
        images = img_low[group * group_rows:(group + 1) * group_rows]
        for offset in range(STEPS + 1):
            source = (group - offset) % N_GRP
            moved_text = txt_low[source * group_rows:(source + 1) * group_rows]
            logits = temp * jnp.dot(images, moved_text.T, preferred_element_type=jnp.float32) + bias
            target = ident if offset == 0 else jnp.zeros_like(ident)
            slopes = (temp * (jax.nn.sigmoid(logits) - target)).astype(jnp.bfloat16)
            grad_u[group] = grad_u[group] + jnp.dot(slopes, moved_text, preferred_element_type=jnp.float32)
            grad_v[source] = grad_v[source] + jnp.dot(slopes.T, images, preferred_element_type=jnp.float32)
    full_u = jnp.concatenate(grad_u, axis=0)
    full_v = jnp.concatenate(grad_v, axis=0)
    return (back_rows(img_unit, img_inv, full_u), back_rows(txt_unit, txt_inv, full_v))
```

```python
import functools

import jax
import jax.numpy as jnp
from jax import lax
from jax.experimental import pallas as pl
from jax.experimental.pallas import tpu as pltpu
from jax.sharding import PartitionSpec as P

X, ZL, ZH, Y, CORE = 4, 2, 4, 4, 2
GROUPS, DEVS = X * ZL, ZH * Y * CORE


def to_group(block, step):
    return lax.ppermute(block, "grp", [(i, (i + step) % GROUPS) for i in range(GROUPS)])


def to_dev(block, zh=0, y=0, core=0):
    route = []
    for i in range(DEVS):
        a, b, c = i // (Y * CORE), i // CORE % Y, i % CORE
        target = ((a + zh) % ZH * Y + (b + y) % Y) * CORE + (c + core) % CORE
        route.append((i, target))
    return lax.ppermute(block, "dev", route)


def unit_rows(values):
    inverse = lax.rsqrt(jnp.sum(values * values, axis=1, keepdims=True) + 1e-06)
    return (values * inverse, inverse)


def back_rows(unit, inverse, upstream):
    return inverse * (upstream - unit * jnp.sum(unit * upstream, axis=1, keepdims=True))


TILE = 512


def pair_kernel(own, scalars, img, txt_sib, txt_own, *refs):
    step = pl.program_id(0)
    half_temp, half_bias = scalars[0], scalars[1]
    if own:
        gu_0, gu_n, gu_2, gv_sib, gv_own, acc, coef = refs
        past_sib = past_own = None
    else:
        past_sib, past_own, gu_0, gu_n, gu_2, gv_sib, gv_own, acc, coef = refs

    def tile(txt, gv, past, first_own):
        logits = lax.dot_general(
            img[...], txt[...], (((1,), (1,)), ((), ())), preferred_element_type=jnp.float32
        )
        slopes = half_temp * jnp.tanh(half_temp * logits + half_bias) + half_temp
        coef[...] = slopes.astype(jnp.bfloat16)
        if own and first_own is not None:

            @pl.when(step == first_own)
            def _():
                rows = lax.broadcasted_iota(jnp.int32, (128, 128), 0)
                cols = lax.broadcasted_iota(jnp.int32, (128, 128), 1)
                lowered = slopes[:128, :128] - jnp.where(rows == cols, 2.0 * half_temp, 0.0)
                coef[:128, :128] = lowered.astype(jnp.bfloat16)

        part = jnp.dot(coef[...], txt[...], preferred_element_type=jnp.float32)

        @pl.when(step == 0)
        def _():
            acc[...] = part

        @pl.when(step > 0)
        def _():
            acc[...] += part

        sums = lax.dot_general(
            coef[...], img[...], (((0,), (0,)), ((), ())), preferred_element_type=jnp.float32
        )
        if past is not None:
            sums = sums + past[...]
        gv[...] = sums.astype(gv.dtype)

    half = pl.num_programs(0) // 2

    @pl.when(step < half)
    def _():
        tile(txt_sib, gv_sib, past_sib, None)

    @pl.when(step >= half)
    def _():
        tile(txt_own, gv_own, past_own, half)

    @pl.when(step == pl.num_programs(0) - 1)
    def _():
        gu_0[...] = acc[0:128].astype(gu_0.dtype)
        gu_n[...] = acc[128:384].astype(gu_n.dtype)
        gu_2[...] = acc[384:512].astype(gu_2.dtype)


def pairs(scalars, img, txt_sib, txt_own, past=None):
    own = past is None
    rows, width = img.shape
    count = txt_own.shape[0]
    half = count // TILE
    kind = jnp.float32 if own else jnp.bfloat16
    sib = pl.BlockSpec((TILE, width), lambda i: (jnp.minimum(i, half - 1), 0))
    mine = pl.BlockSpec((TILE, width), lambda i: (jnp.maximum(i - half, 0), 0))

    def whole(n):
        return pl.BlockSpec((n, width), lambda i: (0, 0))

    return pl.pallas_call(
        functools.partial(pair_kernel, own),
        grid=(2 * half,),
        in_specs=[pl.BlockSpec(memory_space=pltpu.SMEM), whole(rows), sib, mine]
        + ([] if own else [sib, mine]),
        out_specs=[whole(128), whole(256), whole(128), sib, mine],
        out_shape=[
            jax.ShapeDtypeStruct((128, width), kind),
            jax.ShapeDtypeStruct((256, width), kind),
            jax.ShapeDtypeStruct((128, width), kind),
            jax.ShapeDtypeStruct((count, width), kind),
            jax.ShapeDtypeStruct((count, width), jnp.float32),
        ],
        scratch_shapes=[
            pltpu.VMEM((rows, width), jnp.float32),
            pltpu.VMEM((rows, TILE), jnp.bfloat16),
        ],
        compiler_params=pltpu.CompilerParams(vmem_limit_bytes=40 * 1024 * 1024),
        cost_estimate=pl.CostEstimate(
            flops=3 * 2 * rows * 2 * count * width,
            bytes_accessed=2 * count * width * 6,
            transcendentals=rows * 2 * count,
        ),
    )(scalars, img, txt_sib, txt_own, *([] if own else past))


def local(image_emb, text_emb, temp, bias):
    f32, low = jnp.float32, jnp.bfloat16
    img_unit, img_inv = unit_rows(image_emb)
    txt_unit, txt_inv = unit_rows(text_emb)
    img_0 = img_unit.astype(low)
    txt_0 = txt_unit.astype(low)
    scalars = jnp.stack([0.5 * temp, 0.5 * bias])

    txt_behind = to_group(txt_0, 1)
    img_up = to_dev(img_0, zh=-1)
    img_down = to_dev(img_0, zh=1)
    img_2 = to_dev(img_0, zh=2)
    ahead_0 = to_group(img_0, -2)
    img_n = jnp.concatenate([img_up, img_down], axis=0)
    ahead_n = to_group(img_n, -2)
    ahead_2 = to_group(img_2, -2)
    txt_pair = jnp.concatenate([txt_0, txt_behind], axis=0)
    txt_up = to_dev(txt_pair, y=-1)
    txt_down = to_dev(txt_pair, y=1)
    txt_2 = to_dev(txt_pair, y=2)
    txt_own = jnp.concatenate([txt_pair, txt_up, txt_down, txt_2], axis=0)
    txt_sib = to_dev(txt_own, core=1)
    img_own = jnp.concatenate([img_0, img_n, img_2], axis=0)
    img_ahead = jnp.concatenate([ahead_0, ahead_n, ahead_2], axis=0)

    gu_0, gu_n, gu_2, past_sib, past_own = pairs(scalars, img_own, txt_sib, txt_own)
    au_0, au_n, au_2, gv_sib, gv_own = pairs(scalars, img_ahead, txt_sib, txt_own, (past_sib, past_own))

    gu_2 = gu_2 + to_group(au_2, 2).astype(f32)
    gu_n = gu_n + to_group(au_n, 2).astype(f32)
    gu_0 = gu_0 + to_group(au_0, 2).astype(f32)
    gu = (
        gu_0
        + to_dev(gu_2.astype(low), zh=2).astype(f32)
        + to_dev(gu_n[:128].astype(low), zh=1).astype(f32)
        + to_dev(gu_n[128:].astype(low), zh=-1).astype(f32)
    )
    gv_own = gv_own + to_dev(gv_sib, core=1).astype(f32)
    gv_pair = (
        gv_own[:256]
        + to_dev(gv_own[768:].astype(low), y=2).astype(f32)
        + to_dev(gv_own[256:512].astype(low), y=1).astype(f32)
        + to_dev(gv_own[512:768].astype(low), y=-1).astype(f32)
    )
    gv = gv_pair[:128] + to_group(gv_pair[128:].astype(low), -1).astype(f32)
    return (back_rows(img_unit, img_inv, gu), back_rows(txt_unit, txt_inv, gv))


def solution(mesh):
    return jax.shard_map(
        local,
        mesh=mesh,
        in_specs=(P(("grp", "dev"), None), P(("grp", "dev"), None), P(), P()),
        out_specs=(P(("grp", "dev"), None), P(("grp", "dev"), None)),
        check_vma=False,
    )
```

```python
import functools

import jax
import jax.numpy as jnp
from jax import lax
from jax.experimental import pallas as pl
from jax.experimental.pallas import tpu as pltpu
from jax.sharding import PartitionSpec as P

X, ZL, ZH, Y, CORE = 4, 2, 4, 4, 2
GROUPS, DEVS = X * ZL, ZH * Y * CORE


def to_group(block, step):
    return lax.ppermute(block, "grp", [(i, (i + step) % GROUPS) for i in range(GROUPS)])


def to_dev(block, zh=0, y=0, core=0):
    route = []
    for i in range(DEVS):
        a, b, c = i // (Y * CORE), i // CORE % Y, i % CORE
        target = ((a + zh) % ZH * Y + (b + y) % Y) * CORE + (c + core) % CORE
        route.append((i, target))
    return lax.ppermute(block, "dev", route)


def fence(*arrays):
    return lax.optimization_barrier(arrays)


def unit_rows(values):
    inverse = lax.rsqrt(jnp.sum(values * values, axis=1, keepdims=True) + 1e-06)
    return (values * inverse, inverse)


def back_rows(unit, inverse, upstream):
    return inverse * (upstream - unit * jnp.sum(unit * upstream, axis=1, keepdims=True))


TILE = 512


def pair_kernel(own, scalars, img, txt_sib, txt_own, *refs):
    step = pl.program_id(0)
    half_temp, half_bias = scalars[0], scalars[1]
    if own:
        gu_0, gu_n, gu_2, gv_sib, gv_own, acc, coef = refs
        past_sib = past_own = None
    else:
        past_sib, past_own, gu_0, gu_n, gu_2, gv_sib, gv_own, acc, coef = refs

    def tile(txt, gv, past, first_own):
        logits = lax.dot_general(
            img[...], txt[...], (((1,), (1,)), ((), ())), preferred_element_type=jnp.float32
        )
        slopes = half_temp * jnp.tanh(half_temp * logits + half_bias) + half_temp
        coef[...] = slopes.astype(jnp.bfloat16)
        if own and first_own is not None:

            @pl.when(step == first_own)
            def _():
                rows = lax.broadcasted_iota(jnp.int32, (128, 128), 0)
                cols = lax.broadcasted_iota(jnp.int32, (128, 128), 1)
                lowered = slopes[:128, :128] - jnp.where(rows == cols, 2.0 * half_temp, 0.0)
                coef[:128, :128] = lowered.astype(jnp.bfloat16)

        part = jnp.dot(coef[...], txt[...], preferred_element_type=jnp.float32)

        @pl.when(step == 0)
        def _():
            acc[...] = part

        @pl.when(step > 0)
        def _():
            acc[...] += part

        sums = lax.dot_general(
            coef[...], img[...], (((0,), (0,)), ((), ())), preferred_element_type=jnp.float32
        )
        if past is not None:
            sums = sums + past[...]
        gv[...] = sums.astype(gv.dtype)

    half = pl.num_programs(0) // 2

    @pl.when(step < half)
    def _():
        tile(txt_sib, gv_sib, past_sib, None)

    @pl.when(step >= half)
    def _():
        tile(txt_own, gv_own, past_own, half)

    @pl.when(step == pl.num_programs(0) - 1)
    def _():
        gu_0[...] = acc[0:128].astype(gu_0.dtype)
        gu_n[...] = acc[128:384].astype(gu_n.dtype)
        gu_2[...] = acc[384:512].astype(gu_2.dtype)


def pairs(scalars, img, txt_sib, txt_own, past=None):
    own = past is None
    rows, width = img.shape
    count = txt_own.shape[0]
    half = count // TILE
    kind = jnp.float32 if own else jnp.bfloat16
    sib = pl.BlockSpec((TILE, width), lambda i: (jnp.minimum(i, half - 1), 0))
    mine = pl.BlockSpec((TILE, width), lambda i: (jnp.maximum(i - half, 0), 0))

    def whole(n):
        return pl.BlockSpec((n, width), lambda i: (0, 0))

    return pl.pallas_call(
        functools.partial(pair_kernel, own),
        grid=(2 * half,),
        in_specs=[pl.BlockSpec(memory_space=pltpu.SMEM), whole(rows), sib, mine]
        + ([] if own else [sib, mine]),
        out_specs=[whole(128), whole(256), whole(128), sib, mine],
        out_shape=[
            jax.ShapeDtypeStruct((128, width), kind),
            jax.ShapeDtypeStruct((256, width), kind),
            jax.ShapeDtypeStruct((128, width), kind),
            jax.ShapeDtypeStruct((count, width), kind),
            jax.ShapeDtypeStruct((count, width), jnp.float32),
        ],
        scratch_shapes=[
            pltpu.VMEM((rows, width), jnp.float32),
            pltpu.VMEM((rows, TILE), jnp.bfloat16),
        ],
        compiler_params=pltpu.CompilerParams(vmem_limit_bytes=40 * 1024 * 1024),
        cost_estimate=pl.CostEstimate(
            flops=3 * 2 * rows * 2 * count * width,
            bytes_accessed=2 * count * width * 6,
            transcendentals=rows * 2 * count,
        ),
    )(scalars, img, txt_sib, txt_own, *([] if own else past))


def local(image_emb, text_emb, temp, bias):
    f32, low = jnp.float32, jnp.bfloat16
    img_unit, img_inv = unit_rows(image_emb)
    txt_unit, txt_inv = unit_rows(text_emb)
    img_0 = img_unit.astype(low)
    txt_0 = txt_unit.astype(low)
    scalars = jnp.stack([0.5 * temp, 0.5 * bias])

    txt_behind = to_group(txt_0, 1)
    img_up = to_dev(img_0, zh=-1)
    img_down = to_dev(img_0, zh=1)
    ahead_0 = to_group(img_0, -2)
    txt_behind, img_up, img_down, ahead_0 = fence(txt_behind, img_up, img_down, ahead_0)
    txt_pair = jnp.concatenate([txt_0, txt_behind], axis=0)
    img_n = jnp.concatenate([img_up, img_down], axis=0)
    txt_up = to_dev(txt_pair, y=-1)
    txt_down = to_dev(txt_pair, y=1)
    img_2 = to_dev(img_0, zh=2)
    ahead_n = to_group(img_n, -2)
    txt_up, txt_down, img_2, ahead_n = fence(txt_up, txt_down, img_2, ahead_n)
    txt_far_a = to_dev(txt_up[:128], y=-1)
    txt_far_b = to_dev(txt_down[128:], y=1)
    ahead_2 = to_group(img_2, -2)
    txt_near = jnp.concatenate([txt_pair, txt_up, txt_down], axis=0)
    sib_near = to_dev(txt_near, core=1)
    txt_far_a, txt_far_b, ahead_2, sib_near = fence(txt_far_a, txt_far_b, ahead_2, sib_near)
    txt_far = jnp.concatenate([txt_far_a, txt_far_b], axis=0)
    sib_far = to_dev(txt_far, core=1)
    txt_own = jnp.concatenate([txt_near, txt_far], axis=0)
    txt_sib = jnp.concatenate([sib_near, sib_far], axis=0)
    img_own = jnp.concatenate([img_0, img_n, img_2], axis=0)
    img_ahead = jnp.concatenate([ahead_0, ahead_n, ahead_2], axis=0)

    gu_0, gu_n, gu_2, past_sib, past_own = pairs(scalars, img_own, txt_sib, txt_own)
    au_0, au_n, au_2, gv_sib, gv_own = pairs(scalars, img_ahead, txt_sib, txt_own, (past_sib, past_own))

    back_sib = to_dev(gv_sib, core=1)
    back_2 = to_group(au_2, 2)
    back_sib, back_2, au_n = fence(back_sib, back_2, au_n)
    gv_own = gv_own + back_sib.astype(f32)
    gu_2 = (gu_2 + back_2.astype(f32)).astype(low)
    gv_up = to_dev(gv_own[256:512].astype(low), y=1)
    gv_down = to_dev(gv_own[512:768].astype(low), y=-1)
    sum_2 = to_dev(gu_2, zh=2)
    back_n = to_group(au_n, 2)
    gv_up, gv_down, sum_2, back_n, au_0 = fence(gv_up, gv_down, sum_2, back_n, au_0)
    gu_n = (gu_n + back_n.astype(f32)).astype(low)
    gv_2 = to_dev(gv_own[768:].astype(low), y=2)
    sum_up = to_dev(gu_n[:128], zh=1)
    sum_down = to_dev(gu_n[128:], zh=-1)
    back_0 = to_group(au_0, 2)
    gv_2, sum_up, sum_down, back_0 = fence(gv_2, sum_up, sum_down, back_0)
    gv_pair = gv_own[:256] + gv_up.astype(f32) + gv_down.astype(f32) + gv_2.astype(f32)
    gv = gv_pair[:128] + to_group(gv_pair[128:].astype(low), -1).astype(f32)
    gu = gu_0 + back_0.astype(f32) + sum_2.astype(f32) + sum_up.astype(f32) + sum_down.astype(f32)
    return (back_rows(img_unit, img_inv, gu), back_rows(txt_unit, txt_inv, gv))


def solution(mesh):
    return jax.shard_map(
        local,
        mesh=mesh,
        in_specs=(P(("grp", "dev"), None), P(("grp", "dev"), None), P(), P()),
        out_specs=(P(("grp", "dev"), None), P(("grp", "dev"), None)),
        check_vma=False,
    )
```

```python
import functools

import jax
import jax.numpy as jnp
from jax import lax
from jax.experimental import pallas as pl
from jax.experimental.pallas import tpu as pltpu
from jax.sharding import PartitionSpec as P

X, ZL, ZH, Y, CORE = 4, 2, 4, 4, 2
GROUPS, DEVS = X * ZL, ZH * Y * CORE
F32, LOW = jnp.float32, jnp.bfloat16


def to_group(block, step):
    return lax.ppermute(block, "grp", [(i, (i + step) % GROUPS) for i in range(GROUPS)])


def to_dev(block, zh=0, y=0, core=0):
    route = []
    for i in range(DEVS):
        a, b, c = i // (Y * CORE), i // CORE % Y, i % CORE
        target = ((a + zh) % ZH * Y + (b + y) % Y) * CORE + (c + core) % CORE
        route.append((i, target))
    return lax.ppermute(block, "dev", route)


def fence(*arrays):
    return lax.optimization_barrier(arrays)


def unit_rows(values):
    inverse = lax.rsqrt(jnp.sum(values * values, axis=1, keepdims=True) + 1e-06)
    return (values * inverse, inverse)


def back_rows(unit, inverse, upstream):
    return inverse * (upstream - unit * jnp.sum(unit * upstream, axis=1, keepdims=True))


def pair_kernel(count, with_gu, with_gv, diagonal, scalars, img, *refs):
    refs = list(refs)
    txts = [refs.pop(0) for _ in range(count)]
    gu_in = refs.pop(0) if with_gu else None
    gv_in = [refs.pop(0) for _ in range(count)] if with_gv else None
    gu, gvs = refs[0], refs[1 : 1 + count]
    total = refs[1 + count] if len(refs) > 1 + count else gu
    half_temp, half_bias = scalars[0], scalars[1]
    for j, txt in enumerate(txts):
        logits = lax.dot_general(
            img[...], txt[...], (((1,), (1,)), ((), ())), preferred_element_type=F32
        )
        slopes = half_temp * jnp.tanh(half_temp * logits + half_bias) + half_temp
        if diagonal and j == 0:
            rows = lax.broadcasted_iota(jnp.int32, slopes.shape, 0)
            cols = lax.broadcasted_iota(jnp.int32, slopes.shape, 1)
            own = jnp.logical_and(rows == cols, rows < 128)
            slopes = slopes - jnp.where(own, 2.0 * half_temp, 0.0)
        coef = slopes.astype(LOW)
        part = jnp.dot(coef, txt[...], preferred_element_type=F32)
        if j == 0 and with_gu:
            part = part + gu_in[...]
        if j > 0:
            part = part + total[...]
        if j < count - 1:
            total[...] = part
        else:
            gu[...] = part.astype(gu.dtype)
        sums = lax.dot_general(
            coef, img[...], (((0,), (0,)), ((), ())), preferred_element_type=F32
        )
        if with_gv:
            sums = sums + gv_in[j][...]
        gvs[j][...] = sums.astype(gvs[j].dtype)


def pairs(scalars, img, txts, gu_in=None, gv_in=None, gu_kind=F32, gv_kinds=None, diagonal=False):
    count, (rows, width) = len(txts), img.shape
    gv_kinds = gv_kinds or [F32] * count
    each = txts[0].shape[0]
    vmem = pl.BlockSpec(memory_space=pltpu.VMEM)
    operands = [scalars, img, *txts]
    aliases = {}
    if gu_in is not None:
        if gu_kind == F32:
            aliases[len(operands)] = 0
        operands.append(gu_in)
    if gv_in is not None:
        for j in range(count):
            if gv_kinds[j] == F32:
                aliases[len(operands)] = 1 + j
            operands.append(gv_in[j])
    return pl.pallas_call(
        functools.partial(pair_kernel, count, gu_in is not None, gv_in is not None, diagonal),
        in_specs=[pl.BlockSpec(memory_space=pltpu.SMEM)] + [vmem] * (len(operands) - 1),
        out_specs=[vmem] * (1 + count),
        out_shape=[jax.ShapeDtypeStruct((rows, width), gu_kind)]
        + [jax.ShapeDtypeStruct((each, width), kind) for kind in gv_kinds],
        input_output_aliases=aliases,
        scratch_shapes=[] if gu_kind == F32 else [pltpu.VMEM((rows, width), F32)],
        compiler_params=pltpu.CompilerParams(vmem_limit_bytes=28 * 1024 * 1024),
        cost_estimate=pl.CostEstimate(
            flops=3 * 2 * rows * count * each * width,
            bytes_accessed=count * each * width * 6,
            transcendentals=rows * count * each,
        ),
    )(*operands)


def local(image_emb, text_emb, temp, bias):
    img_unit, img_inv = unit_rows(image_emb)
    txt_unit, txt_inv = unit_rows(text_emb)
    img_0 = img_unit.astype(LOW)
    txt_0 = txt_unit.astype(LOW)
    scalars = jnp.stack([0.5 * temp, 0.5 * bias])

    behind_0 = to_group(txt_0, 1)
    img_up = to_dev(img_0, zh=-1)
    img_down = to_dev(img_0, zh=1)
    ahead_0 = to_group(img_0, -2)
    txt_up = to_dev(txt_0, y=-1)
    txt_down = to_dev(txt_0, y=1)
    txt_2 = to_dev(txt_0, y=2)
    behind_0, img_up, img_down, ahead_0, txt_up, txt_down, txt_2 = fence(
        behind_0, img_up, img_down, ahead_0, txt_up, txt_down, txt_2
    )
    img_n = jnp.concatenate([img_up, img_down], axis=0)
    own_c = jnp.concatenate([txt_0, txt_up, txt_down, txt_2], axis=0)
    img_2 = to_dev(img_0, zh=2)
    ahead_n = to_group(img_n, -2)
    behind_up = to_dev(behind_0, y=-1)
    behind_down = to_dev(behind_0, y=1)
    behind_2 = to_dev(behind_0, y=2)
    own_s = to_dev(own_c, core=1)
    img_2, ahead_n, behind_up, behind_down, behind_2, own_s = fence(
        img_2, ahead_n, behind_up, behind_down, behind_2, own_s
    )
    img_own = jnp.concatenate([img_0, img_n, img_2], axis=0)
    ahead_2 = to_group(img_2, -2)
    sh_c = jnp.concatenate([behind_0, behind_up, behind_down, behind_2], axis=0)
    sh_s = to_dev(sh_c, core=1)
    gu_own, *gv_o = pairs(scalars, img_own, [own_c, own_s], diagonal=True)
    gu_own, *gv_s = pairs(scalars, img_own, [sh_c, sh_s], gu_in=gu_own)
    ahead_2, gu_own = fence(ahead_2, gu_own)

    texts = [sh_c, sh_s, own_c, own_s]
    sums = [*gv_s, *gv_o]
    au_2, *sums = pairs(scalars, ahead_2, texts, gv_in=sums, gu_kind=LOW)
    back_2 = to_group(au_2, 2)
    au_n, *sums = pairs(scalars, ahead_n, texts, gv_in=sums, gu_kind=LOW)
    back_n = to_group(au_n, 2)
    au_0, sh_mine, sh_theirs, own_mine, own_theirs = pairs(
        scalars, ahead_0, texts, gv_in=sums, gu_kind=LOW, gv_kinds=[F32, LOW, F32, LOW]
    )
    back_0 = to_group(au_0, 2)
    sh_got = to_dev(sh_theirs, core=1)
    own_got = to_dev(own_theirs, core=1)
    back_2, sh_got, own_got = fence(back_2, sh_got, own_got)
    sh_mine = sh_mine + sh_got.astype(F32)
    own_mine = own_mine + own_got.astype(F32)
    sh_up = to_dev(sh_mine[128:256].astype(LOW), y=1)
    sh_down = to_dev(sh_mine[256:384].astype(LOW), y=-1)
    sh_2 = to_dev(sh_mine[384:].astype(LOW), y=2)
    sum_2 = to_dev((gu_own[384:] + back_2.astype(F32)).astype(LOW), zh=2)
    sh_up, sh_down, sh_2, sum_2, back_n = fence(sh_up, sh_down, sh_2, sum_2, back_n)
    near = (gu_own[128:384] + back_n.astype(F32)).astype(LOW)
    sum_up = to_dev(near[:128], zh=1)
    sum_down = to_dev(near[128:], zh=-1)
    own_up = to_dev(own_mine[128:256].astype(LOW), y=1)
    own_down = to_dev(own_mine[256:384].astype(LOW), y=-1)
    own_2 = to_dev(own_mine[384:].astype(LOW), y=2)
    sh_sum = sh_mine[:128] + sh_up.astype(F32) + sh_down.astype(F32) + sh_2.astype(F32)
    gv_behind = to_group(sh_sum.astype(LOW), -1)
    gu = gu_own[:128] + back_0.astype(F32) + sum_2.astype(F32) + sum_up.astype(F32) + sum_down.astype(F32)
    gv = own_mine[:128] + own_up.astype(F32) + own_down.astype(F32) + own_2.astype(F32) + gv_behind.astype(F32)
    return (back_rows(img_unit, img_inv, gu), back_rows(txt_unit, txt_inv, gv))


def solution(mesh):
    return jax.shard_map(
        local,
        mesh=mesh,
        in_specs=(P(("grp", "dev"), None), P(("grp", "dev"), None), P(), P()),
        out_specs=(P(("grp", "dev"), None), P(("grp", "dev"), None)),
        check_vma=False,
    )
```

```python
import functools

import jax
import jax.numpy as jnp
from jax import lax
from jax.experimental import pallas as pl
from jax.experimental.pallas import tpu as pltpu
from jax.sharding import PartitionSpec as P

X, ZL, ZH, Y, CORE = 4, 2, 4, 4, 2
GROUPS, DEVS = X * ZL, ZH * Y * CORE
F32, LOW = jnp.float32, jnp.bfloat16


def to_group(block, step):
    return lax.ppermute(block, "grp", [(i, (i + step) % GROUPS) for i in range(GROUPS)])


def to_dev(block, zh=0, y=0, core=0):
    route = []
    for i in range(DEVS):
        a, b, c = i // (Y * CORE), i // CORE % Y, i % CORE
        target = ((a + zh) % ZH * Y + (b + y) % Y) * CORE + (c + core) % CORE
        route.append((i, target))
    return lax.ppermute(block, "dev", route)


def fence(*arrays):
    return lax.optimization_barrier(arrays)


def unit_rows(values):
    inverse = lax.rsqrt(jnp.sum(values * values, axis=1, keepdims=True) + 1e-06)
    return (values * inverse, inverse)


def back_rows(unit, inverse, upstream):
    return inverse * (upstream - unit * jnp.sum(unit * upstream, axis=1, keepdims=True))


def pair_kernel(plan, scalars, *refs):
    images, texts, tiles, gu_past, gv_past, diagonal = plan
    refs = list(refs)
    imgs = [refs.pop(0) for _ in range(images)]
    txts = [refs.pop(0) for _ in range(texts)]
    gu_in = [refs.pop(0) if past else None for past in gu_past]
    gv_in = [refs.pop(0) if past else None for past in gv_past]
    gus = [refs.pop(0) for _ in range(images)]
    gvs = [refs.pop(0) for _ in range(texts)]
    totals = [gu if gu.dtype == F32 else refs.pop(0) for gu in gus]
    half_temp, half_bias = scalars[0], scalars[1]
    for n, (j, first, size) in enumerate(tiles):
        span = pl.ds(first, size)
        txt = txts[j][span]
        sums = None if gv_in[j] is None else gv_in[j][span]
        for m, img in enumerate(imgs):
            logits = lax.dot_general(
                img[...], txt, (((1,), (1,)), ((), ())), preferred_element_type=F32
            )
            slopes = half_temp * jnp.tanh(half_temp * logits + half_bias) + half_temp
            if diagonal and m == 0 and n == 0:
                rows = lax.broadcasted_iota(jnp.int32, slopes.shape, 0)
                cols = lax.broadcasted_iota(jnp.int32, slopes.shape, 1)
                own = jnp.logical_and(rows == cols, rows < 128)
                slopes = slopes - jnp.where(own, 2.0 * half_temp, 0.0)
            coef = slopes.astype(LOW)
            part = jnp.dot(coef, txt, preferred_element_type=F32)
            if n > 0:
                part = part + totals[m][...]
            elif gu_in[m] is not None:
                part = part + gu_in[m][...]
            if n < len(tiles) - 1:
                totals[m][...] = part
            else:
                gus[m][...] = part.astype(gus[m].dtype)
            term = lax.dot_general(
                coef, img[...], (((0,), (0,)), ((), ())), preferred_element_type=F32
            )
            sums = term if sums is None else sums + term
        gvs[j][span] = sums.astype(gvs[j].dtype)


def pairs(scalars, imgs, txts, gu_in=None, gv_in=None, gu_kinds=None, gv_kinds=None, diagonal=False):
    width = imgs[0].shape[1]
    gu_in, gv_in = gu_in or [None] * len(imgs), gv_in or [None] * len(txts)
    gu_kinds, gv_kinds = gu_kinds or [F32] * len(imgs), gv_kinds or [F32] * len(txts)
    tiles = []
    for j, txt in enumerate(txts):
        for first in range(0, txt.shape[0], 512):
            tiles.append((j, first, min(512, txt.shape[0] - first)))
    operands, aliases = [scalars, *imgs, *txts], {}
    for place, (past, kind) in enumerate(zip(gu_in + gv_in, gu_kinds + gv_kinds)):
        if past is not None:
            if kind == F32:
                aliases[len(operands)] = place
            operands.append(past)
    plan = (
        len(imgs),
        len(txts),
        tiles,
        [past is not None for past in gu_in],
        [past is not None for past in gv_in],
        diagonal,
    )
    rows, cols = sum(i.shape[0] for i in imgs), sum(t.shape[0] for t in txts)
    vmem = pl.BlockSpec(memory_space=pltpu.VMEM)
    return pl.pallas_call(
        functools.partial(pair_kernel, plan),
        in_specs=[pl.BlockSpec(memory_space=pltpu.SMEM)] + [vmem] * (len(operands) - 1),
        out_specs=[vmem] * (len(imgs) + len(txts)),
        out_shape=[jax.ShapeDtypeStruct(i.shape, kind) for i, kind in zip(imgs, gu_kinds)]
        + [jax.ShapeDtypeStruct(t.shape, kind) for t, kind in zip(txts, gv_kinds)],
        input_output_aliases=aliases,
        scratch_shapes=[pltpu.VMEM(i.shape, F32) for i, kind in zip(imgs, gu_kinds) if kind != F32],
        compiler_params=pltpu.CompilerParams(vmem_limit_bytes=28 * 1024 * 1024),
        cost_estimate=pl.CostEstimate(
            flops=3 * 2 * rows * cols * width,
            bytes_accessed=cols * width * 6,
            transcendentals=rows * cols,
        ),
    )(*operands)


def local(image_emb, text_emb, temp, bias):
    txt_unit, txt_inv = unit_rows(text_emb)
    img_unit, img_inv = unit_rows(image_emb)
    img_0, txt_0 = fence(img_unit.astype(LOW), txt_unit.astype(LOW))
    scalars = jnp.stack([0.5 * temp, 0.5 * bias])

    txt_2 = to_dev(txt_0, y=2)
    ahead_0 = to_group(img_0, -2)
    img_up = to_dev(img_0, zh=-1)
    img_down = to_dev(img_0, zh=1)
    behind_0 = to_group(txt_0, 1)
    txt_2, ahead_0, img_up, img_down, behind_0 = fence(txt_2, ahead_0, img_up, img_down, behind_0)
    pair_0 = jnp.concatenate([txt_0, behind_0], axis=0)
    img_n = jnp.concatenate([img_up, img_down], axis=0)
    pair_up = to_dev(pair_0, y=-1)
    pair_down = to_dev(pair_0, y=1)
    ahead_n = to_group(img_n, -2)
    img_2 = to_dev(img_0, zh=2)
    pair_up, pair_down, ahead_n, img_2 = fence(pair_up, pair_down, ahead_n, img_2)
    txt_c = jnp.concatenate(
        [txt_0, pair_up[:128], pair_down[:128], txt_2, behind_0, pair_up[128:], pair_down[128:]], axis=0
    )
    img_own = jnp.concatenate([img_0, img_n, img_2], axis=0)
    txt_s = to_dev(txt_c, core=1)
    far_c = to_dev(behind_0, y=2)
    ahead_2 = to_group(img_2, -2)
    gu_own, gv_c = pairs(scalars, [img_own], [txt_c], diagonal=True)
    gu_own, gv_s = pairs(scalars, [img_own], [txt_s], gu_in=[gu_own])
    far_c, ahead_2, gu_own, gv_s = fence(far_c, ahead_2, gu_own, gv_s)
    far_s = to_dev(far_c, core=1)
    img_ahead = jnp.concatenate([ahead_0, ahead_n, ahead_2], axis=0)
    gu_ahead, gv_c, gv_s = pairs(
        scalars, [img_ahead], [txt_c, txt_s], gv_in=[gv_c, gv_s], gv_kinds=[F32, LOW]
    )
    got = to_dev(gv_s, core=1)
    far = jnp.concatenate([far_c, far_s], axis=0)
    gu_own, gu_ahead, gv_far = pairs(
        scalars, [img_own, img_ahead], [far], gu_in=[gu_own, gu_ahead], gu_kinds=[F32, LOW]
    )
    got, gv_far, gu_ahead = fence(got, gv_far, gu_ahead)
    gv_c = gv_c + got.astype(F32)
    far_got = to_dev(gv_far[128:].astype(LOW), core=1)
    sh_up = to_dev(gv_c[640:768].astype(LOW), y=1)
    sh_down = to_dev(gv_c[768:].astype(LOW), y=-1)
    back_2 = to_group(gu_ahead[384:], 2)
    far_got, sh_up, sh_down, back_2, gu_near, gv_near = fence(
        far_got, sh_up, sh_down, back_2, gu_ahead[128:384], gv_c[128:384].astype(LOW)
    )
    far_sum = to_dev((gv_far[:128] + far_got.astype(F32)).astype(LOW), y=2)
    own_up = to_dev(gv_near[:128], y=1)
    own_down = to_dev(gv_near[128:], y=-1)
    back_n = to_group(gu_near, 2)
    sum_2 = to_dev((gu_own[384:] + back_2.astype(F32)).astype(LOW), zh=2)
    far_sum, own_up, own_down, back_n, sum_2, gu_first, gv_last = fence(
        far_sum, own_up, own_down, back_n, sum_2, gu_ahead[:128], gv_c[384:512].astype(LOW)
    )
    near = (gu_own[128:384] + back_n.astype(F32)).astype(LOW)
    behind = gv_c[512:640] + sh_up.astype(F32) + sh_down.astype(F32) + far_sum.astype(F32)
    own_far = to_dev(gv_last, y=2)
    back_0 = to_group(gu_first, 2)
    sum_up = to_dev(near[:128], zh=1)
    sum_down = to_dev(near[128:], zh=-1)
    gv_behind = to_group(behind.astype(LOW), -1)
    own_far, back_0, sum_up, sum_down, gv_behind = fence(own_far, back_0, sum_up, sum_down, gv_behind)
    gu = gu_own[:128] + back_0.astype(F32) + sum_2.astype(F32) + sum_up.astype(F32) + sum_down.astype(F32)
    gv = gv_c[:128] + own_up.astype(F32) + own_down.astype(F32) + own_far.astype(F32) + gv_behind.astype(F32)
    return (back_rows(img_unit, img_inv, gu), back_rows(txt_unit, txt_inv, gv))


def solution(mesh):
    return jax.shard_map(
        local,
        mesh=mesh,
        in_specs=(P(("grp", "dev"), None), P(("grp", "dev"), None), P(), P()),
        out_specs=(P(("grp", "dev"), None), P(("grp", "dev"), None)),
        check_vma=False,
    )
```

```python
import functools

import jax
import jax.numpy as jnp
from jax import lax
from jax.experimental import pallas as pl
from jax.experimental.pallas import tpu as pltpu
from jax.sharding import PartitionSpec as P

X, ZL, ZH, Y, CORE = 4, 2, 4, 4, 2
GROUPS, DEVS = X * ZL, ZH * Y * CORE
F32, LOW = jnp.float32, jnp.bfloat16


def to_group(block, step):
    return lax.ppermute(block, "grp", [(i, (i + step) % GROUPS) for i in range(GROUPS)])


def to_dev(block, zh=0, y=0, core=0):
    route = []
    for i in range(DEVS):
        a, b, c = i // (Y * CORE), i // CORE % Y, i % CORE
        target = ((a + zh) % ZH * Y + (b + y) % Y) * CORE + (c + core) % CORE
        route.append((i, target))
    return lax.ppermute(block, "dev", route)


def fence(*arrays):
    return lax.optimization_barrier(arrays)


VMEM = pl.BlockSpec(memory_space=pltpu.VMEM)
TILE = 512


def whole(kernel, outs, *operands, flops=0, scalars=False, aliases=None, scratch=()):
    first = [pl.BlockSpec(memory_space=pltpu.SMEM)] if scalars else [VMEM]
    size = sum(int(o.size) * o.dtype.itemsize for o in operands)
    return pl.pallas_call(
        kernel,
        in_specs=first + [VMEM] * (len(operands) - 1),
        out_specs=[VMEM] * len(outs),
        out_shape=[jax.ShapeDtypeStruct(shape, kind) for shape, kind in outs],
        input_output_aliases=aliases or {},
        scratch_shapes=list(scratch),
        compiler_params=pltpu.CompilerParams(vmem_limit_bytes=28 * 1024 * 1024),
        cost_estimate=pl.CostEstimate(flops=flops, bytes_accessed=size, transcendentals=0),
    )(*operands)


def inverse_of(values):
    return lax.rsqrt(jnp.sum(values * values, axis=1, keepdims=True) + 1e-06)


def unit_kernel(txt, img, txt_low, img_low):
    for values, low in ((txt, txt_low), (img, img_low)):
        low[...] = (values[...] * inverse_of(values[...])).astype(LOW)


def end_kernel(img, txt, gu_0, *refs):
    *parts, gv_0, up, down, far, behind, grad_img, grad_txt = refs
    gu = gu_0[0:128]
    for part in parts:
        gu = gu + part[...].astype(F32)
    gv = gv_0[0:128]
    for part in (up, down, far, behind):
        gv = gv + part[...].astype(F32)
    for values, sums, grad in ((img, gu, grad_img), (txt, gv, grad_txt)):
        inverse = inverse_of(values[...])
        unit = values[...] * inverse
        grad[...] = inverse * (sums - unit * jnp.sum(unit * sums, axis=1, keepdims=True))


def text_sums_kernel(mine, got, keep, sh_up, sh_down, sh_far, own_up, own_down, own_far):
    def rows(n):
        return mine[pl.ds(n * 128, 128)] + got[pl.ds(n * 128, 128)].astype(F32)

    keep[0:128] = rows(0)
    keep[128:256] = rows(4)
    for n, out in ((1, own_up), (2, own_down), (3, own_far), (5, sh_up), (6, sh_down), (7, sh_far)):
        out[...] = rows(n).astype(LOW)


def pair_kernel(gu_past, gv_past, diagonal, parts, scalars, img, txt, *refs):
    refs = list(refs)
    gu_in = refs.pop(0) if gu_past else None
    gv_in = refs.pop(0) if gv_past else None
    gus = [refs.pop(0) for _ in parts]
    gv = refs.pop(0)
    total = refs.pop(0) if refs else gus[0]
    half_temp, half_bias = scalars[0], scalars[1]
    if gu_past and total is not gus[0]:
        total[...] = gu_in[...]

    @pl.loop(0, txt.shape[0] // TILE)
    def _(n):
        first = pl.multiple_of(n * TILE, TILE)
        span = pl.ds(first, TILE)
        logits = lax.dot_general(
            img[...], txt[span], (((1,), (1,)), ((), ())), preferred_element_type=F32
        )
        slopes = half_temp * jnp.tanh(half_temp * logits + half_bias) + half_temp
        if diagonal:
            rows = lax.broadcasted_iota(jnp.int32, slopes.shape, 0)
            cols = lax.broadcasted_iota(jnp.int32, slopes.shape, 1) + first
            own = jnp.logical_and(rows == cols, rows < 128)
            slopes = slopes - jnp.where(own, 2.0 * half_temp, 0.0)
        coef = slopes.astype(LOW)
        part = jnp.dot(coef, txt[span], preferred_element_type=F32)
        if gu_past:
            total[...] += part
        else:

            @pl.when(n == 0)
            def _():
                total[...] = part

            @pl.when(n > 0)
            def _():
                total[...] += part

        term = lax.dot_general(
            coef, img[...], (((0,), (0,)), ((), ())), preferred_element_type=F32
        )
        if gv_past:
            term = term + gv_in[span]
        gv[span] = term.astype(gv.dtype)

    if total is not gus[0]:
        for (first, size), out in zip(parts, gus):
            out[...] = total[first : first + size].astype(out.dtype)


def pairs(scalars, img, txt, gu_in=None, gv_in=None, gu_parts=None, gv_kind=F32, diagonal=False):
    (rows, width), cols = img.shape, txt.shape[0]
    operands, aliases = [scalars, img, txt], {}
    parts, kind, scratch = gu_parts or [(0, rows)], F32, []
    if gu_parts:
        kind, scratch = LOW, [pltpu.VMEM((rows, width), F32)]
    if gu_in is not None:
        if not gu_parts:
            aliases[len(operands)] = 0
        operands.append(gu_in)
    if gv_in is not None:
        if gv_kind == F32:
            aliases[len(operands)] = len(parts)
        operands.append(gv_in)
    outs = [((size, width), kind) for _, size in parts] + [((cols, width), gv_kind)]
    kernel = functools.partial(pair_kernel, gu_in is not None, gv_in is not None, diagonal, parts)
    return whole(
        kernel,
        outs,
        *operands,
        flops=6 * rows * cols * width,
        scalars=True,
        aliases=aliases,
        scratch=scratch,
    )


def local(image_emb, text_emb, temp, bias):
    rows = image_emb.shape
    txt_0, img_0 = whole(unit_kernel, [(rows, LOW)] * 2, text_emb, image_emb)
    scalars = jnp.stack([0.5 * temp, 0.5 * bias])

    txt_2 = to_dev(txt_0, y=2)
    ahead_0 = to_group(img_0, -2)
    img_up = to_dev(img_0, zh=-1)
    img_down = to_dev(img_0, zh=1)
    behind_0 = to_group(txt_0, 1)
    txt_2, ahead_0, img_up, img_down, behind_0 = fence(txt_2, ahead_0, img_up, img_down, behind_0)
    pair_0 = jnp.concatenate([txt_0, behind_0], axis=0)
    img_n = jnp.concatenate([img_up, img_down], axis=0)
    pair_0, img_n, behind_0, img_0 = fence(pair_0, img_n, behind_0, img_0)
    behind_2 = to_dev(behind_0, y=2)
    pair_up = to_dev(pair_0, y=-1)
    pair_down = to_dev(pair_0, y=1)
    ahead_n = to_group(img_n, -2)
    img_2 = to_dev(img_0, zh=2)
    behind_2, pair_up, pair_down, ahead_n, img_2 = fence(behind_2, pair_up, pair_down, ahead_n, img_2)
    txt_c = jnp.concatenate(
        [txt_0, pair_up[:128], pair_down[:128], txt_2, behind_0, pair_up[128:], pair_down[128:], behind_2],
        axis=0,
    )
    img_own = jnp.concatenate([img_0, img_n, img_2], axis=0)
    txt_s = to_dev(txt_c, core=1)
    ahead_2 = to_group(img_2, -2)
    gu_own, gv_c = pairs(scalars, img_own, txt_c, diagonal=True)
    gu_own, gv_s = pairs(scalars, img_own, txt_s, gu_in=gu_own)
    ahead_2, gu_own, gv_s = fence(ahead_2, gu_own, gv_s)
    img_ahead = jnp.concatenate([ahead_0, ahead_n, ahead_2], axis=0)
    gu_ahead, gv_s = pairs(scalars, img_ahead, txt_s, gv_in=gv_s, gv_kind=LOW)
    got = to_dev(gv_s, core=1)
    au_0, au_n, au_2, gv_c = pairs(
        scalars, img_ahead, txt_c, gu_in=gu_ahead, gv_in=gv_c, gu_parts=[(0, 128), (128, 256), (384, 128)]
    )
    got, gv_c, au_2 = fence(got, gv_c, au_2)
    gv_keep, sh_up, sh_down, sh_far, own_up, own_down, own_far = whole(
        text_sums_kernel, [((256, rows[1]), F32)] + [(rows, LOW)] * 6, gv_c, got
    )
    sh_up = to_dev(sh_up, y=1)
    sh_down = to_dev(sh_down, y=-1)
    back_2 = to_group(au_2, 2)
    sh_up, sh_down, back_2, au_n, sh_far, own_up, own_down = fence(
        sh_up, sh_down, back_2, au_n, sh_far, own_up, own_down
    )
    sum_2 = (gu_own[384:] + back_2.astype(F32)).astype(LOW)
    sum_2, au_n, sh_far, own_up, own_down = fence(sum_2, au_n, sh_far, own_up, own_down)
    sh_far = to_dev(sh_far, y=2)
    own_up = to_dev(own_up, y=1)
    own_down = to_dev(own_down, y=-1)
    back_n = to_group(au_n, 2)
    sum_2 = to_dev(sum_2, zh=2)
    sh_far, own_up, own_down, back_n, sum_2, au_0, own_far = fence(
        sh_far, own_up, own_down, back_n, sum_2, au_0, own_far
    )
    sum_up = (gu_own[128:256] + back_n[:128].astype(F32)).astype(LOW)
    sum_down = (gu_own[256:384] + back_n[128:].astype(F32)).astype(LOW)
    behind = (gv_keep[128:] + sh_up.astype(F32) + sh_down.astype(F32) + sh_far.astype(F32)).astype(LOW)
    sum_up, sum_down, behind, au_0, own_far = fence(sum_up, sum_down, behind, au_0, own_far)
    own_far = to_dev(own_far, y=2)
    back_0 = to_group(au_0, 2)
    behind = to_group(behind, -1)
    sum_up = to_dev(sum_up, zh=1)
    sum_down = to_dev(sum_down, zh=-1)
    return tuple(
        whole(
            end_kernel,
            [(rows, F32)] * 2,
            image_emb,
            text_emb,
            gu_own,
            back_0,
            sum_2,
            sum_up,
            sum_down,
            gv_keep,
            own_up,
            own_down,
            own_far,
            behind,
        )
    )


def solution(mesh):
    return jax.shard_map(
        local,
        mesh=mesh,
        in_specs=(P(("grp", "dev"), None), P(("grp", "dev"), None), P(), P()),
        out_specs=(P(("grp", "dev"), None), P(("grp", "dev"), None)),
        check_vma=False,
    )
```

```python
import functools

import jax
import jax.numpy as jnp
from jax import lax
from jax.experimental import pallas as pl
from jax.experimental.pallas import tpu as pltpu
from jax.sharding import PartitionSpec as P

X, ZL, ZH, Y, CORE = 4, 2, 4, 4, 2
GROUPS, DEVS = X * ZL, ZH * Y * CORE
F32, LOW = jnp.float32, jnp.bfloat16


def to_group(block, step):
    return lax.ppermute(block, "grp", [(i, (i + step) % GROUPS) for i in range(GROUPS)])


def to_dev(block, zh=0, y=0, core=0):
    route = []
    for i in range(DEVS):
        a, b, c = i // (Y * CORE), i // CORE % Y, i % CORE
        target = ((a + zh) % ZH * Y + (b + y) % Y) * CORE + (c + core) % CORE
        route.append((i, target))
    return lax.ppermute(block, "dev", route)


def fence(*arrays):
    return lax.optimization_barrier(arrays)


VMEM = pl.BlockSpec(memory_space=pltpu.VMEM)


def whole(kernel, outs, *operands, scalars=False, aliases=None, scratch=()):
    first = [pl.BlockSpec(memory_space=pltpu.SMEM)] if scalars else [VMEM]
    return pl.pallas_call(
        kernel,
        in_specs=first + [VMEM] * (len(operands) - 1),
        out_specs=[VMEM] * len(outs),
        out_shape=[jax.ShapeDtypeStruct(shape, kind) for shape, kind in outs],
        input_output_aliases=aliases or {},
        scratch_shapes=list(scratch),
        compiler_params=pltpu.CompilerParams(vmem_limit_bytes=28 * 1024 * 1024),
        cost_estimate=pl.CostEstimate(flops=1, bytes_accessed=1, transcendentals=0),
    )(*operands)


def inverse_of(values):
    return lax.rsqrt(jnp.sum(values * values, axis=1, keepdims=True) + 1e-06)


def each(rows, step):
    def over(body):
        @pl.loop(0, rows // step)
        def _(n):
            body(pl.ds(pl.multiple_of(n * step, step), step))

    return over


def unit_kernel(txt, img, txt_low, img_low):
    for values, low in ((txt, txt_low), (img, img_low)):

        @each(values.shape[0], 32)
        def _(span):
            low[span] = (values[span] * inverse_of(values[span])).astype(LOW)


def end_kernel(img, txt, gu_0, *refs):
    *parts, gv_0, up, down, far, behind, grad_img, grad_txt = refs
    sides = ((img, gu_0, parts, grad_img), (txt, gv_0, (up, down, far, behind), grad_txt))
    for values, own, others, grad in sides:

        @each(values.shape[0], 32)
        def _(span):
            sums = own[span]
            for other in others:
                sums = sums + other[span].astype(F32)
            inverse = inverse_of(values[span])
            unit = values[span] * inverse
            grad[span] = inverse * (sums - unit * jnp.sum(unit * sums, axis=1, keepdims=True))


def text_sums_kernel(mine, got, own_0, sh_0, sh_up, sh_down, sh_far, own_up, own_down, own_far):
    for n, out in enumerate((own_0, own_up, own_down, own_far, sh_0, sh_up, sh_down, sh_far)):

        @each(out.shape[0], 32)
        def _(span):
            there = pl.ds(pl.multiple_of(n * out.shape[0] + span.start, 32), 32)
            out[span] = (mine[there] + got[there].astype(F32)).astype(out.dtype)


def products(scalars, img, txt, mask=None):
    half_temp, half_bias = scalars[0], scalars[1]
    logits = lax.dot_general(img, txt, (((1,), (1,)), ((), ())), preferred_element_type=F32)
    slopes = half_temp * jnp.tanh(half_temp * logits + half_bias) + half_temp
    if mask is not None:
        slopes = slopes - jnp.where(mask, 2.0 * half_temp, 0.0)
    coef = slopes.astype(LOW)
    gu = jnp.dot(coef, txt, preferred_element_type=F32)
    return gu, lax.dot_general(coef, img, (((0,), (0,)), ((), ())), preferred_element_type=F32)


def pair_kernel(gu_past, gv_past, diagonal, parts, scalars, img, txt_c, txt_s, *refs):
    refs = list(refs)
    gu_in = refs.pop(0) if gu_past else None
    gv_in = refs.pop(0) if gv_past else None
    gus = [refs.pop(0) for _ in parts]
    gv, txt = refs[:2]
    total = refs[2] if len(refs) > 2 else gus[0]
    if total is not gus[0] or not gu_past:

        @each(total.shape[0], 32)
        def _(span):
            total[span] = gu_in[span] if gu_past else jnp.zeros((32, total.shape[1]), F32)

    @pl.loop(0, 2)
    def _(n):
        for place, side in enumerate((txt_c, txt_s)):

            @pl.when(n == place)
            def _():
                @each(txt.shape[0], 32)
                def _(span):
                    txt[span] = side[span]

        mask = None
        if diagonal:
            rows = lax.broadcasted_iota(jnp.int32, (img.shape[0], txt.shape[0]), 0)
            cols = lax.broadcasted_iota(jnp.int32, (img.shape[0], txt.shape[0]), 1) + n * img.shape[0]
            mask = jnp.logical_and(rows == cols, rows < 128)
        part, term = products(scalars, img[...], txt[...], mask)
        total[...] += part
        span = pl.ds(pl.multiple_of(n * txt.shape[0], txt.shape[0]), txt.shape[0])
        if gv_past:
            term = term + gv_in[span]
        gv[span] = term

    if total is not gus[0]:
        for (first, size, _), out in zip(parts, gus):

            @each(size, 32)
            def _(span):
                there = pl.ds(pl.multiple_of(first + span.start, 32), 32)
                out[span] = total[there].astype(out.dtype)


def pairs(scalars, img, txt_c, txt_s, gu_in=None, gv_in=None, gu_parts=None, diagonal=False):
    (rows, width), cols = img.shape, txt_c.shape[0]
    operands, aliases = [scalars, img, txt_c, txt_s], {}
    parts = gu_parts or [(0, rows, F32)]
    scratch = [pltpu.VMEM((cols, width), LOW)]
    if gu_parts:
        scratch.append(pltpu.VMEM((rows, width), F32))
    if gu_in is not None:
        if not gu_parts:
            aliases[len(operands)] = 0
        operands.append(gu_in)
    if gv_in is not None:
        aliases[len(operands)] = len(parts)
        operands.append(gv_in)
    outs = [((size, width), kind) for _, size, kind in parts] + [((2 * cols, width), F32)]
    kernel = functools.partial(pair_kernel, gu_in is not None, gv_in is not None, diagonal, parts)
    return whole(
        kernel,
        outs,
        *operands,
        scalars=True,
        aliases=aliases,
        scratch=scratch,
    )


def last_kernel(place, scalars, img, own, sh, gv_own, gv_sh, *refs):
    gu_in, (gu, gv) = (refs[0] if len(refs) > 2 else None), refs[-2:]
    size = own.shape[0]
    total = None if gu_in is None else gu_in[...]
    for n, (txt, past) in enumerate(((own, gv_own), (sh, gv_sh))):
        part, term = products(scalars, img[...], txt[...])
        total = part if total is None else total + part
        gv[n * size : (n + 1) * size] = (term + past[place : place + size]).astype(gv.dtype)
    gu[...] = total.astype(gu.dtype)


def local(image_emb, text_emb, temp, bias):
    rows = image_emb.shape
    txt_0, img_0 = whole(unit_kernel, [(rows, LOW)] * 2, text_emb, image_emb)
    scalars = jnp.stack([0.5 * temp, 0.5 * bias])

    txt_up = to_dev(txt_0, y=-1)
    ahead_0 = to_group(img_0, -2)
    img_up = to_dev(img_0, zh=-1)
    img_down = to_dev(img_0, zh=1)
    behind_0 = to_group(txt_0, 1)
    ahead_0, txt_later = fence(ahead_0, txt_0)
    txt_down = to_dev(txt_later, y=1)
    txt_2 = to_dev(txt_later, y=2)
    txt_up, txt_down, txt_2, img_up, img_down, behind_0 = fence(
        txt_up, txt_down, txt_2, img_up, img_down, behind_0
    )
    own_c = jnp.concatenate([txt_0, txt_up, txt_down, txt_2], axis=0)
    img_n = jnp.concatenate([img_up, img_down], axis=0)
    first = jnp.concatenate([img_0, img_up, img_down, ahead_0], axis=0)
    own_s = to_dev(own_c, core=1)
    behind_up = to_dev(behind_0, y=-1)
    behind_down = to_dev(behind_0, y=1)
    ahead_n = to_group(img_n, -2)
    img_2 = to_dev(img_0, zh=2)
    own_s, behind_later = fence(own_s, behind_0)
    behind_2 = to_dev(behind_later, y=2)
    gu_first, gv_own = pairs(scalars, first, own_c, own_s, diagonal=True)
    behind_up, behind_down, behind_2, ahead_n, img_2, gu_first, gv_own = fence(
        behind_up, behind_down, behind_2, ahead_n, img_2, gu_first, gv_own
    )
    sh_c = jnp.concatenate([behind_0, behind_up, behind_down, behind_2], axis=0)
    second = jnp.concatenate([img_2, ahead_n], axis=0)
    sh_s = to_dev(sh_c, core=1)
    ahead_2 = to_group(img_2, -2)
    gu_second, gv_own = pairs(scalars, second, own_c, own_s, gv_in=gv_own)
    gu_2, au_n, gv_sh = pairs(
        scalars, second, sh_c, sh_s, gu_in=gu_second, gu_parts=[(0, 128, F32), (128, 256, LOW)]
    )
    back_n = to_group(au_n, 2)
    gu_0, gu_up, gu_down, au_0, gv_sh = pairs(
        scalars,
        first,
        sh_c,
        sh_s,
        gu_in=gu_first,
        gv_in=gv_sh,
        gu_parts=[(0, 128, F32), (128, 128, F32), (256, 128, F32), (384, 128, LOW)],
    )
    ahead_2, gv_sh = fence(ahead_2, gv_sh)
    wide = (2 * own_c.shape[0], rows[1])
    gu_last, gv_s = whole(
        functools.partial(last_kernel, own_c.shape[0]),
        [(rows, F32), (wide, LOW)],
        *(scalars, ahead_2, own_s, sh_s, gv_own, gv_sh),
        scalars=True,
    )
    got = to_dev(gv_s, core=1)
    au_2, gv_c = whole(
        functools.partial(last_kernel, 0),
        [(rows, LOW), (wide, F32)],
        *(scalars, ahead_2, own_c, sh_c, gv_own, gv_sh, gu_last),
        scalars=True,
    )
    got, back_n, au_2, gv_c = fence(got, back_n, au_2, gv_c)
    own_sum, sh_sum, sh_up, sh_down, sh_far, own_up, own_down, own_far = whole(
        text_sums_kernel, [(rows, F32)] * 2 + [(rows, LOW)] * 6, gv_c, got
    )
    sum_up = (gu_up + back_n[:128].astype(F32)).astype(LOW)
    sum_down = (gu_down + back_n[128:].astype(F32)).astype(LOW)
    sum_up, sum_down, sh_up, sh_down, au_2 = fence(sum_up, sum_down, sh_up, sh_down, au_2)
    back_2 = to_group(au_2, 2)
    sh_up = to_dev(sh_up, y=1)
    sh_down = to_dev(sh_down, y=-1)
    sum_up = to_dev(sum_up, zh=1)
    sum_down = to_dev(sum_down, zh=-1)
    back_2, sh_far = fence(back_2, sh_far)
    sh_far = to_dev(sh_far, y=2)
    sum_up, sum_down, back_2, sh_up, sh_down, sh_far, au_0, own_up, own_down = fence(
        sum_up, sum_down, back_2, sh_up, sh_down, sh_far, au_0, own_up, own_down
    )
    sum_2 = (gu_2 + back_2.astype(F32)).astype(LOW)
    behind = (sh_sum + sh_up.astype(F32) + sh_down.astype(F32) + sh_far.astype(F32)).astype(LOW)
    sum_2, behind, au_0, own_up, own_down = fence(sum_2, behind, au_0, own_up, own_down)
    back_0 = to_group(au_0, 2)
    own_up = to_dev(own_up, y=1)
    own_down = to_dev(own_down, y=-1)
    behind = to_group(behind, -1)
    sum_2 = to_dev(sum_2, zh=2)
    back_0, own_far = fence(back_0, own_far)
    own_far = to_dev(own_far, y=2)
    return tuple(
        whole(
            end_kernel,
            [(rows, F32)] * 2,
            *(image_emb, text_emb, gu_0, back_0, sum_2, sum_up, sum_down),
            *(own_sum, own_up, own_down, own_far, behind),
        )
    )


def solution(mesh):
    return jax.shard_map(
        local,
        mesh=mesh,
        in_specs=(P(("grp", "dev"), None), P(("grp", "dev"), None), P(), P()),
        out_specs=(P(("grp", "dev"), None), P(("grp", "dev"), None)),
        check_vma=False,
    )
```

```python
import functools

import jax
import jax.numpy as jnp
from jax import lax
from jax.experimental import pallas as pl
from jax.experimental.pallas import tpu as pltpu
from jax.sharding import PartitionSpec as P

X, ZL, ZH, Y, CORE = 4, 2, 4, 4, 2
GROUPS, DEVS = X * ZL, ZH * Y * CORE
F32, LOW = jnp.float32, jnp.bfloat16


def to_group(block, step):
    return lax.ppermute(block, "grp", [(i, (i + step) % GROUPS) for i in range(GROUPS)])


def to_dev(block, zh=0, y=0, core=0):
    route = []
    for i in range(DEVS):
        a, b, c = i // (Y * CORE), i // CORE % Y, i % CORE
        target = ((a + zh) % ZH * Y + (b + y) % Y) * CORE + (c + core) % CORE
        route.append((i, target))
    return lax.ppermute(block, "dev", route)


def fence(*arrays):
    return lax.optimization_barrier(arrays)


VMEM = pl.BlockSpec(memory_space=pltpu.VMEM)


def whole(kernel, outs, *operands, scalars=False, aliases=None, scratch=()):
    first = [pl.BlockSpec(memory_space=pltpu.SMEM)] if scalars else [VMEM]
    return pl.pallas_call(
        kernel,
        in_specs=first + [VMEM] * (len(operands) - 1),
        out_specs=[VMEM] * len(outs),
        out_shape=[jax.ShapeDtypeStruct(shape, kind) for shape, kind in outs],
        input_output_aliases=aliases or {},
        scratch_shapes=list(scratch),
        compiler_params=pltpu.CompilerParams(vmem_limit_bytes=28 * 1024 * 1024),
        cost_estimate=pl.CostEstimate(flops=1, bytes_accessed=1, transcendentals=0),
    )(*operands)


def inverse_of(values):
    return lax.rsqrt(jnp.sum(values * values, axis=1, keepdims=True) + 1e-06)


def each(rows, step):
    def over(body):
        @pl.loop(0, rows // step)
        def _(n):
            body(pl.ds(pl.multiple_of(n * step, step), step))

    return over


def unit_kernel(txt, img, txt_low, img_low):
    for values, low in ((txt, txt_low), (img, img_low)):

        @each(values.shape[0], 32)
        def _(span):
            low[span] = (values[span] * inverse_of(values[span])).astype(LOW)


def end_kernel(img, txt, gu_0, *refs):
    *parts, gv_0, up, down, far, behind, grad_img, grad_txt = refs
    sides = ((img, gu_0, parts, grad_img), (txt, gv_0, (up, down, far, behind), grad_txt))
    for values, own, others, grad in sides:

        @each(values.shape[0], 32)
        def _(span):
            sums = own[span]
            for other in others:
                sums = sums + other[span].astype(F32)
            inverse = inverse_of(values[span])
            unit = values[span] * inverse
            grad[span] = inverse * (sums - unit * jnp.sum(unit * sums, axis=1, keepdims=True))


def text_sums_kernel(place, mine, got_0, got_1, own, up, down, far):
    for n, out in enumerate((own, up, down, far)):

        @each(128, 32)
        def _(span):
            there = pl.ds(pl.multiple_of(place + n * 128 + span.start, 32), 32)
            inside = pl.ds(pl.multiple_of(n % 2 * 128 + span.start, 32), 32)
            got = (got_0, got_1)[n // 2]
            out[span] = (mine[there] + got[inside].astype(F32)).astype(out.dtype)


def products(scalars, img, txt, mask=None):
    half_temp, half_bias = scalars[0], scalars[1]
    logits = lax.dot_general(img, txt, (((1,), (1,)), ((), ())), preferred_element_type=F32)
    slopes = half_temp * jnp.tanh(half_temp * logits + half_bias) + half_temp
    if mask is not None:
        slopes = slopes - jnp.where(mask, 2.0 * half_temp, 0.0)
    coef = slopes.astype(LOW)
    gu = jnp.dot(coef, txt, preferred_element_type=F32)
    return gu, lax.dot_general(coef, img, (((0,), (0,)), ((), ())), preferred_element_type=F32)


def first_kernel(scalars, img_0, img_n, ahead_0, txt, gu, gv, img):
    for part, first in ((img_0, 0), (img_n, 128), (ahead_0, 384), (ahead_0, 512)):

        @each(part.shape[0], 32)
        def _(span):
            img[pl.ds(pl.multiple_of(first + span.start, 32), 32)] = part[span]

    shape = gu.shape[0], txt.shape[0]
    row, col = lax.broadcasted_iota(jnp.int32, shape, 0), lax.broadcasted_iota(jnp.int32, shape, 1)
    mask = jnp.logical_and(row == col, row < 128)
    gu[...], gv[: shape[1]] = products(scalars, img[0 : shape[0]], txt[...], mask)

    @each(shape[1], 32)
    def _(span):
        there = pl.ds(pl.multiple_of(shape[1] + span.start, 32), 32)
        gv[there] = jnp.zeros((32, gv.shape[1]), F32)


def both_halves(txt):
    size = txt.shape[0] // 2

    def over(body):
        @pl.loop(0, 2)
        def _(n):
            body(n, pl.ds(pl.multiple_of(n * size, size), size))

    return over


def second_kernel(scalars, img, txt, gv_in, gu, gv):
    @each(gu.shape[0], 32)
    def _(span):
        gu[span] = jnp.zeros((32, gu.shape[1]), F32)

    @both_halves(txt)
    def _(n, here):
        part, term = products(scalars, img[...], txt[here])
        gu[...] += part
        gv[here] = term + gv_in[here]


def third_kernel(scalars, img, txt, gu_in, gu_2, gu_n, gv, gu):
    @each(gu.shape[0], 32)
    def _(span):
        gu[span] = gu_in[span]

    @both_halves(txt)
    def _(n, here):
        part, gv[here] = products(scalars, img[...], txt[here])
        gu[...] += part

    gu_2[...] = gu[:128]
    gu_n[:256] = gu[128:].astype(LOW)
    gu_n[256:] = jnp.zeros((16, gu_n.shape[1]), LOW)


def fourth_kernel(scalars, img, txt, gu_in, gv_in, gu, piece_0, piece_1, piece_2, piece_3, gv):
    past = gu_in.shape[0]

    @each(past, 32)
    def _(span):
        gu[span] = gu_in[span]

    @each(gu.shape[0] - past, 32)
    def _(span):
        there = pl.ds(pl.multiple_of(past + span.start, 32), 32)
        gu[there] = jnp.zeros((32, gu.shape[1]), F32)

    @both_halves(txt)
    def _(n, here):
        part, term = products(scalars, img[...], txt[here])
        gu[...] += part
        gv[...] = term + gv_in[here]
        for place, outs in enumerate(((piece_0, piece_1), (piece_2, piece_3))):

            @pl.when(n == place)
            def _():
                for m, out in enumerate(outs):

                    @each(256, 32)
                    def _(span):
                        there = pl.ds(pl.multiple_of(m * 256 + span.start, 32), 32)
                        out[span] = gv[there].astype(LOW)


def fifth_kernel(scalars, img, txt, gu_in, gv_in, gu_0, gu_up, gu_down, au_0, au_2, gv, gu):
    size, past = txt.shape[0] // 2, img.shape[0] - 128
    part, term = products(scalars, img[...], txt[size:])
    gu[...] = gu_in[...] + part
    gv[size:] = term + gv_in[size:]
    part, term = products(scalars, img[past:], txt[0:size])
    gu[past:] += part
    gv[:size] = term + gv_in[:size]
    for n, out in enumerate((gu_0, gu_up, gu_down, au_0, au_2)):

        @each(128, 32)
        def _(span):
            out[span] = gu[pl.ds(pl.multiple_of(n * 128 + span.start, 32), 32)].astype(out.dtype)


def local(image_emb, text_emb, temp, bias):
    rows = image_emb.shape
    txt_0, img_0 = whole(unit_kernel, [(rows, LOW)] * 2, text_emb, image_emb)
    scalars = jnp.stack([0.5 * temp, 0.5 * bias])

    txt_up = to_dev(txt_0, y=-1)
    ahead_0 = to_group(img_0, -2)
    img_up = to_dev(img_0, zh=-1)
    img_down = to_dev(img_0, zh=1)
    behind_0 = to_group(txt_0, 1)
    ahead_0, txt_later = fence(ahead_0, txt_0)
    txt_down = to_dev(txt_later, y=1)
    txt_2 = to_dev(txt_later, y=2)
    txt_up, txt_down, txt_2, img_up, img_down, behind_0 = fence(
        txt_up, txt_down, txt_2, img_up, img_down, behind_0
    )
    width = rows[1]
    own_c = jnp.concatenate([txt_0, txt_up, txt_down, txt_2], axis=0)
    img_n = jnp.concatenate([img_up, img_down], axis=0)
    own_c, img_n, behind_0, img_0 = fence(own_c, img_n, behind_0, img_0)
    behind_up = to_dev(behind_0, y=-1)
    behind_down = to_dev(behind_0, y=1)
    behind_2 = to_dev(behind_0, y=2)
    ahead_n = to_group(img_n, -2)
    img_2 = to_dev(img_0, zh=2)
    half, wide = (own_c.shape[0], width), (2 * own_c.shape[0], width)
    gu_first, sums_c, images = whole(
        first_kernel,
        [(half, F32), (wide, F32), ((640, width), LOW)],
        *(scalars, img_0, img_n, ahead_0, own_c),
        scalars=True,
    )
    behind_up, behind_down, behind_2, ahead_n, img_2, gu_first, sums_c = fence(
        behind_up, behind_down, behind_2, ahead_n, img_2, gu_first, sums_c
    )
    txt_c = jnp.concatenate([own_c, behind_0, behind_up, behind_down, behind_2], axis=0)
    second = jnp.concatenate([img_2, ahead_n], axis=0)
    txt_s = to_dev(txt_c, core=1)
    ahead_2 = to_group(img_2, -2)
    gu_second, sums_c = whole(
        second_kernel,
        [(second.shape, F32), (wide, F32)],
        *(scalars, second, txt_c, sums_c),
        scalars=True,
        aliases={3: 1},
    )
    gu_2, au_n, others = whole(
        third_kernel,
        [(rows, F32), ((272, width), LOW), (wide, F32)],
        *(scalars, second, txt_s, gu_second),
        scalars=True,
        scratch=[pltpu.VMEM(second.shape, F32)],
    )
    back_n = to_group(au_n, 2)
    images = lax.dynamic_update_slice(images, ahead_2, (half[0], 0))
    gu_all, *pieces = whole(
        fourth_kernel,
        [(images.shape, F32)] + [((256, width), LOW)] * 4,
        *(scalars, images, txt_s, gu_first, others),
        scalars=True,
        scratch=[pltpu.VMEM(half, F32)],
    )
    got = [to_dev(piece, core=1) for piece in pieces]
    gu_0, gu_up, gu_down, au_0, au_2, sums_c = whole(
        fifth_kernel,
        [(rows, F32)] * 3 + [(rows, LOW)] * 2 + [(wide, F32)],
        *(scalars, images, txt_c, gu_all, sums_c),
        scalars=True,
        aliases={4: 5},
        scratch=[pltpu.VMEM(images.shape, F32)],
    )
    back_n, *got, au_2, sums_c = fence(back_n, *got, au_2, sums_c)
    sums = [(rows, F32)] + [(rows, LOW)] * 3
    sh_sum, sh_up, sh_down, sh_far = whole(
        functools.partial(text_sums_kernel, half[0]), sums, sums_c, *got[2:]
    )
    sum_up = (gu_up + back_n[:128].astype(F32)).astype(LOW)
    sum_down = (gu_down + back_n[128:256].astype(F32)).astype(LOW)
    sum_up, sum_down, sh_up, sh_down, au_2 = fence(sum_up, sum_down, sh_up, sh_down, au_2)
    back_2 = to_group(au_2, 2)
    sh_up = to_dev(sh_up, y=1)
    sh_down = to_dev(sh_down, y=-1)
    sum_up = to_dev(sum_up, zh=1)
    sum_down = to_dev(sum_down, zh=-1)
    back_2, sh_far = fence(back_2, sh_far)
    sh_far = to_dev(sh_far, y=2)
    own_sum, own_up, own_down, own_far = whole(
        functools.partial(text_sums_kernel, 0), sums, sums_c, *got[:2]
    )
    sum_up, sum_down, back_2, sh_up, sh_down, sh_far, au_0, own_up, own_down = fence(
        sum_up, sum_down, back_2, sh_up, sh_down, sh_far, au_0, own_up, own_down
    )
    sum_2 = (gu_2 + back_2.astype(F32)).astype(LOW)
    behind = (sh_sum + sh_up.astype(F32) + sh_down.astype(F32) + sh_far.astype(F32)).astype(LOW)
    sum_2, behind, au_0, own_up, own_down = fence(sum_2, behind, au_0, own_up, own_down)
    back_0 = to_group(au_0, 2)
    own_up = to_dev(own_up, y=1)
    own_down = to_dev(own_down, y=-1)
    behind = to_group(behind, -1)
    sum_2 = to_dev(sum_2, zh=2)
    back_0, own_far = fence(back_0, own_far)
    own_far = to_dev(own_far, y=2)
    return tuple(
        whole(
            end_kernel,
            [(rows, F32)] * 2,
            *(image_emb, text_emb, gu_0, back_0, sum_2, sum_up, sum_down),
            *(own_sum, own_up, own_down, own_far, behind),
        )
    )


def solution(mesh):
    return jax.shard_map(
        local,
        mesh=mesh,
        in_specs=(P(("grp", "dev"), None), P(("grp", "dev"), None), P(), P()),
        out_specs=(P(("grp", "dev"), None), P(("grp", "dev"), None)),
        check_vma=False,
    )
```

```python
import functools

import jax
import jax.numpy as jnp
from jax import lax
from jax.experimental import pallas as pl
from jax.experimental.pallas import tpu as pltpu
from jax.sharding import PartitionSpec as P

X, ZL, ZH, Y, CORE = 4, 2, 4, 4, 2
GROUPS, DEVS = X * ZL, ZH * Y * CORE
F32, LOW = jnp.float32, jnp.bfloat16


def to_group(block, step):
    return lax.ppermute(block, "grp", [(i, (i + step) % GROUPS) for i in range(GROUPS)])


def to_dev(block, zh=0, y=0, core=0):
    route = []
    for i in range(DEVS):
        a, b, c = i // (Y * CORE), i // CORE % Y, i % CORE
        target = ((a + zh) % ZH * Y + (b + y) % Y) * CORE + (c + core) % CORE
        route.append((i, target))
    return lax.ppermute(block, "dev", route)


def fence(*arrays):
    return lax.optimization_barrier(arrays)


VMEM = pl.BlockSpec(memory_space=pltpu.VMEM)


def whole(kernel, outs, *operands, scalars=False, aliases=None, scratch=(), place=pltpu.VMEM, room=28):
    spec = pl.BlockSpec(memory_space=place)
    first = [pl.BlockSpec(memory_space=pltpu.SMEM)] if scalars else [spec]
    return pl.pallas_call(
        kernel,
        in_specs=first + [spec] * (len(operands) - 1),
        out_specs=[VMEM] * len(outs),
        out_shape=[jax.ShapeDtypeStruct(shape, kind) for shape, kind in outs],
        input_output_aliases=aliases or {},
        scratch_shapes=list(scratch),
        compiler_params=pltpu.CompilerParams(vmem_limit_bytes=room * 1024 * 1024),
        cost_estimate=pl.CostEstimate(flops=1, bytes_accessed=1, transcendentals=0),
    )(*operands)


def inverse_of(values):
    return lax.rsqrt(jnp.sum(values * values, axis=1, keepdims=True) + 1e-06)


def each(rows, step):
    def over(body):
        @pl.loop(0, rows // step)
        def _(n):
            body(pl.ds(pl.multiple_of(n * step, step), step))

    return over


def unit_kernel(txt, img, txt_low, img_low, txt_here, img_here, arrived):
    copies = []
    for n, (there, here) in enumerate(((txt, txt_here), (img, img_here))):
        copies.append(pltpu.make_async_copy(there, here, arrived.at[n]))
        copies[-1].start()
    for copy, values, low in ((copies[0], txt_here, txt_low), (copies[1], img_here, img_low)):
        copy.wait()

        @each(values.shape[0], 64)
        def _(span):
            low[span] = (values[span] * inverse_of(values[span])).astype(LOW)


def end_kernel(values, own, *refs):
    *others, grad = refs

    @each(values.shape[0], 64)
    def _(span):
        sums = own[span]
        for other in others:
            sums = sums + other[span].astype(F32)
        inverse = inverse_of(values[span])
        unit = values[span] * inverse
        grad[span] = inverse * (sums - unit * jnp.sum(unit * sums, axis=1, keepdims=True))


def join_kernel(txt_0, txt_up, txt_down, txt_2, img_0, img_up, img_down, own_c, img_n, img_again):
    places = (
        *((own_c, 128 * n, part) for n, part in enumerate((txt_0, txt_up, txt_down, txt_2))),
        *((img_n, 128 * n, part) for n, part in enumerate((img_up, img_down))),
        (img_again, 0, img_0),
    )
    for out, first, part in places:

        @each(128, 64)
        def _(span):
            out[pl.ds(pl.multiple_of(first + span.start, 64), 64)] = part[span]


def text_sums_kernel(place, mine, got_0, got_1, own, up, down, far):
    for n, out in enumerate((own, up, down, far)):

        @each(128, 32)
        def _(span):
            there = pl.ds(pl.multiple_of(place + n * 128 + span.start, 32), 32)
            inside = pl.ds(pl.multiple_of(n % 2 * 128 + span.start, 32), 32)
            got = (got_0, got_1)[n // 2]
            out[span] = (mine[there] + got[inside].astype(F32)).astype(out.dtype)


def products(scalars, img, txt, mask=None):
    half_temp, half_bias = scalars[0], scalars[1]
    logits = lax.dot_general(img, txt, (((1,), (1,)), ((), ())), preferred_element_type=F32)
    slopes = half_temp * jnp.tanh(half_temp * logits + half_bias) + half_temp
    if mask is not None:
        slopes = slopes - jnp.where(mask, 2.0 * half_temp, 0.0)
    coef = slopes.astype(LOW)
    gu = jnp.dot(coef, txt, preferred_element_type=F32)
    return gu, lax.dot_general(coef, img, (((0,), (0,)), ((), ())), preferred_element_type=F32)


def first_kernel(scalars, img_0, img_n, ahead_0, txt, gu, gv, img):
    for part, first in ((img_0, 0), (img_n, 128), (ahead_0, 384)):

        @each(part.shape[0], 32)
        def _(span):
            img[pl.ds(pl.multiple_of(first + span.start, 32), 32)] = part[span]

    shape = gu.shape[0], txt.shape[0]
    row, col = lax.broadcasted_iota(jnp.int32, shape, 0), lax.broadcasted_iota(jnp.int32, shape, 1)
    mask = jnp.logical_and(row == col, row < 128)
    gu[...], gv[: shape[1]] = products(scalars, img[0 : shape[0]], txt[...], mask)

    @each(shape[1], 32)
    def _(span):
        there = pl.ds(pl.multiple_of(shape[1] + span.start, 32), 32)
        gv[there] = jnp.zeros((32, gv.shape[1]), F32)


def both_halves(txt):
    size = txt.shape[0] // 2

    def over(body):
        @pl.loop(0, 2)
        def _(n):
            body(n, pl.ds(pl.multiple_of(n * size, size), size))

    return over


def second_kernel(scalars, img, txt, gv_in, gu, gv):
    @each(gu.shape[0], 32)
    def _(span):
        gu[span] = jnp.zeros((32, gu.shape[1]), F32)

    @both_halves(txt)
    def _(n, here):
        part, term = products(scalars, img[...], txt[here])
        gu[...] += part
        gv[here] = term + gv_in[here]


def third_kernel(scalars, img, txt, gu_in, gu_n, gv, gu):
    @each(gu.shape[0], 32)
    def _(span):
        gu[span] = gu_in[span]

    @both_halves(txt)
    def _(n, here):
        part, gv[here] = products(scalars, img[...], txt[here])
        gu[...] += part

    gu_n[:256] = gu[...].astype(LOW)
    gu_n[256:] = jnp.zeros((16, gu_n.shape[1]), LOW)


def fourth_kernel(scalars, img, txt, gu_in, gv_in, gu, piece_0, piece_1, piece_2, piece_3, gv):
    past = gu_in.shape[0]

    @each(past, 32)
    def _(span):
        gu[span] = gu_in[span]

    @each(gu.shape[0] - past, 32)
    def _(span):
        there = pl.ds(pl.multiple_of(past + span.start, 32), 32)
        gu[there] = jnp.zeros((32, gu.shape[1]), F32)

    @both_halves(txt)
    def _(n, here):
        part, term = products(scalars, img[...], txt[here])
        gu[...] += part
        gv[...] = term + gv_in[here]
        for place, outs in enumerate(((piece_0, piece_1), (piece_2, piece_3))):

            @pl.when(n == place)
            def _():
                for m, out in enumerate(outs):

                    @each(256, 32)
                    def _(span):
                        there = pl.ds(pl.multiple_of(m * 256 + span.start, 32), 32)
                        out[span] = gv[there].astype(LOW)


def fifth_kernel(scalars, img, txt, gu_in, gv_in, gu_0, gu_up, gu_down, gu_2, au, gv, gu):
    size, past = txt.shape[0] // 2, img.shape[0] - 256
    part, term = products(scalars, img[...], txt[size:])
    gu[...] = gu_in[...] + part
    gv[size:] = term + gv_in[size:]
    part, term = products(scalars, img[past:], txt[0:size])
    gu[past:] += part
    gv[:size] = term + gv_in[:size]
    places = (gu_0, 0), (gu_up, 0), (gu_down, 0), (au, 0), (gu_2, 0), (au, 128)
    for n, (out, first) in enumerate(places):

        @each(128, 32)
        def _(span):
            rows = gu[pl.ds(pl.multiple_of(n * 128 + span.start, 32), 32)]
            out[pl.ds(pl.multiple_of(first + span.start, 32), 32)] = rows.astype(out.dtype)


def local(image_emb, text_emb, temp, bias):
    rows = image_emb.shape
    width = rows[1]
    pair, half, wide = (256, width), (512, width), (1024, width)
    here = [pltpu.VMEM(rows, F32)] * 2 + [pltpu.SemaphoreType.DMA((2,))]
    txt_0, img_0 = whole(unit_kernel, [(rows, LOW)] * 2, text_emb, image_emb, place=pltpu.HBM, scratch=here, room=62)
    scalars = jnp.stack([0.5 * temp, 0.5 * bias])

    txt_up = to_dev(txt_0, y=-1)
    ahead_0 = to_group(img_0, -2)
    img_up = to_dev(img_0, zh=-1)
    img_down = to_dev(img_0, zh=1)
    behind_0 = to_group(txt_0, 1)
    ahead_0, txt_later = fence(ahead_0, txt_0)
    txt_down = to_dev(txt_later, y=1)
    txt_2 = to_dev(txt_later, y=2)
    txt_up, txt_down, txt_2, behind_0, img_up, img_down = fence(
        txt_up, txt_down, txt_2, behind_0, img_up, img_down
    )
    own_c, img_n, img_again = whole(
        join_kernel,
        [(half, LOW), (pair, LOW), (rows, LOW)],
        *(txt_0, txt_up, txt_down, txt_2, img_0, img_up, img_down),
    )
    own_c, img_n, behind_0, img_again = fence(own_c, img_n, behind_0, img_again)
    behind_up = to_dev(behind_0, y=-1)
    behind_down = to_dev(behind_0, y=1)
    behind_2 = to_dev(behind_0, y=2)
    ahead_n = to_group(img_n, -2)
    img_2 = to_dev(img_again, zh=2)
    gu_first, sums_c, images = whole(
        first_kernel,
        [(half, F32), (wide, F32), ((768, width), LOW)],
        *(scalars, img_again, img_n, ahead_0, own_c),
        scalars=True,
    )
    behind_up, behind_down, behind_2, ahead_n, img_2, gu_first, sums_c = fence(
        behind_up, behind_down, behind_2, ahead_n, img_2, gu_first, sums_c
    )
    txt_c = jnp.concatenate([own_c, behind_0, behind_up, behind_down, behind_2], axis=0)
    txt_s = to_dev(txt_c, core=1)
    ahead_2 = to_group(img_2, -2)
    gu_n, sums_c = whole(
        second_kernel,
        [(pair, F32), (wide, F32)],
        *(scalars, ahead_n, txt_c, sums_c),
        scalars=True,
        aliases={3: 1},
    )
    au_n, others = whole(
        third_kernel,
        [((272, width), LOW), (wide, F32)],
        *(scalars, ahead_n, txt_s, gu_n),
        scalars=True,
        scratch=[pltpu.VMEM(pair, F32)],
    )
    back_n = to_group(au_n, 2)
    images = lax.dynamic_update_slice(images, jnp.concatenate([img_2, ahead_2], axis=0), (512, 0))
    gu_all, *pieces = whole(
        fourth_kernel,
        [(images.shape, F32)] + [(pair, LOW)] * 4,
        *(scalars, images, txt_s, gu_first, others),
        scalars=True,
        scratch=[pltpu.VMEM(half, F32)],
    )
    got = [to_dev(piece, core=1) for piece in pieces]
    gu_0, gu_up, gu_down, gu_2, au, sums_c = whole(
        fifth_kernel,
        [(rows, F32)] * 4 + [(pair, LOW), (wide, F32)],
        *(scalars, images, txt_c, gu_all, sums_c),
        scalars=True,
        aliases={4: 5},
        scratch=[pltpu.VMEM(images.shape, F32)],
    )
    back_n, *got, au, sums_c = fence(back_n, *got, au, sums_c)
    sums = [(rows, F32)] + [(rows, LOW)] * 3
    sh_sum, sh_up, sh_down, sh_far = whole(
        functools.partial(text_sums_kernel, 512), sums, sums_c, *got[2:]
    )
    sum_up = (gu_up + back_n[:128].astype(F32)).astype(LOW)
    sum_down = (gu_down + back_n[128:256].astype(F32)).astype(LOW)
    sum_up, sum_down, sh_up, sh_down, au = fence(sum_up, sum_down, sh_up, sh_down, au)
    sh_up = to_dev(sh_up, y=1)
    sum_up = to_dev(sum_up, zh=1)
    sum_down = to_dev(sum_down, zh=-1)
    sh_down = to_dev(sh_down, y=-1)
    back = to_group(au, 2)
    sh_up, sh_far = fence(sh_up, sh_far)
    sh_far = to_dev(sh_far, y=2)
    own_sum, own_up, own_down, own_far = whole(
        functools.partial(text_sums_kernel, 0), sums, sums_c, *got[:2]
    )
    sh_up, sum_up, sum_down, sh_down, back, sh_far, own_up, own_down, own_far = fence(
        sh_up, sum_up, sum_down, sh_down, back, sh_far, own_up, own_down, own_far
    )
    back_0, sum_2 = back[:128], (gu_2 + back[128:].astype(F32)).astype(LOW)
    behind = (sh_sum + sh_up.astype(F32) + sh_down.astype(F32) + sh_far.astype(F32)).astype(LOW)
    sum_2, behind, own_up, own_down, own_far = fence(sum_2, behind, own_up, own_down, own_far)
    sum_2 = to_dev(sum_2, zh=2)
    behind = to_group(behind, -1)
    own_up = to_dev(own_up, y=1)
    own_down = to_dev(own_down, y=-1)
    own_far = to_dev(own_far, y=2)
    (grad_image,) = whole(end_kernel, [(rows, F32)], image_emb, gu_0, sum_2, sum_up, sum_down, back_0)
    (grad_text,) = whole(end_kernel, [(rows, F32)], text_emb, own_sum, behind, own_up, own_down, own_far)
    return grad_image, grad_text


def solution(mesh):
    return jax.shard_map(
        local,
        mesh=mesh,
        in_specs=(P(("grp", "dev"), None), P(("grp", "dev"), None), P(), P()),
        out_specs=(P(("grp", "dev"), None), P(("grp", "dev"), None)),
        check_vma=False,
    )
```

```python
import functools

import jax
import jax.numpy as jnp
from jax import lax
from jax.experimental import pallas as pl
from jax.experimental.pallas import tpu as pltpu
from jax.sharding import PartitionSpec as P

X, ZL, ZH, Y, CORE = 4, 2, 4, 4, 2
GROUPS, DEVS = X * ZL, ZH * Y * CORE
F32, LOW = jnp.float32, jnp.bfloat16


def to_group(block, step):
    return lax.ppermute(block, "grp", [(i, (i + step) % GROUPS) for i in range(GROUPS)])


def to_dev(block, zh=0, y=0, core=0):
    route = []
    for i in range(DEVS):
        a, b, c = i // (Y * CORE), i // CORE % Y, i % CORE
        target = ((a + zh) % ZH * Y + (b + y) % Y) * CORE + (c + core) % CORE
        route.append((i, target))
    return lax.ppermute(block, "dev", route)


def fence(*arrays):
    return lax.optimization_barrier(arrays)


VMEM = pl.BlockSpec(memory_space=pltpu.VMEM)


def whole(kernel, outs, *operands, scalars=False, aliases=None, scratch=()):
    first = [pl.BlockSpec(memory_space=pltpu.SMEM)] if scalars else [VMEM]
    return pl.pallas_call(
        kernel,
        in_specs=first + [VMEM] * (len(operands) - 1),
        out_specs=[VMEM] * len(outs),
        out_shape=[jax.ShapeDtypeStruct(shape, kind) for shape, kind in outs],
        input_output_aliases=aliases or {},
        scratch_shapes=list(scratch),
        compiler_params=pltpu.CompilerParams(vmem_limit_bytes=28 * 1024 * 1024),
        cost_estimate=pl.CostEstimate(flops=1, bytes_accessed=1, transcendentals=0),
    )(*operands)


def inverse_of(values):
    return lax.rsqrt(jnp.sum(values * values, axis=1, keepdims=True) + 1e-06)


def each(rows, step):
    def over(body):
        @pl.loop(0, rows // step)
        def _(n):
            body(pl.ds(pl.multiple_of(n * step, step), step))

    return over


def unit_kernel(values, low):
    @each(values.shape[0], 64)
    def _(span):
        low[span] = (values[span] * inverse_of(values[span])).astype(LOW)


def end_kernel(values, own, *refs):
    *others, grad = refs

    @each(values.shape[0], 64)
    def _(span):
        sums = own[span]
        for other in others:
            sums = sums + other[span].astype(F32)
        inverse = inverse_of(values[span])
        unit = values[span] * inverse
        grad[span] = inverse * (sums - unit * jnp.sum(unit * sums, axis=1, keepdims=True))


def join_kernel(txt_0, txt_up, txt_down, txt_2, img_0, img_up, img_down, own_c, img_n, img_again):
    places = (
        *((own_c, 128 * n, part) for n, part in enumerate((txt_0, txt_up, txt_down, txt_2))),
        *((img_n, 128 * n, part) for n, part in enumerate((img_up, img_down))),
        (img_again, 0, img_0),
    )
    for out, first, part in places:

        @each(128, 64)
        def _(span):
            out[pl.ds(pl.multiple_of(first + span.start, 64), 64)] = part[span]


def text_sums_kernel(place, mine, got_0, got_1, own, up, down, far):
    for n, out in enumerate((own, up, down, far)):

        @each(128, 32)
        def _(span):
            there = pl.ds(pl.multiple_of(place + n * 128 + span.start, 32), 32)
            inside = pl.ds(pl.multiple_of(n % 2 * 128 + span.start, 32), 32)
            got = (got_0, got_1)[n // 2]
            out[span] = (mine[there] + got[inside].astype(F32)).astype(out.dtype)


def products(scalars, img, txt, mask=None):
    half_temp, half_bias = scalars[0], scalars[1]
    logits = lax.dot_general(img, txt, (((1,), (1,)), ((), ())), preferred_element_type=F32)
    slopes = half_temp * jnp.tanh(half_temp * logits + half_bias) + half_temp
    if mask is not None:
        slopes = slopes - jnp.where(mask, 2.0 * half_temp, 0.0)
    coef = slopes.astype(LOW)
    gu = jnp.dot(coef, txt, preferred_element_type=F32)
    return gu, lax.dot_general(coef, img, (((0,), (0,)), ((), ())), preferred_element_type=F32)


def first_kernel(scalars, img_0, img_n, ahead_0, txt, gu, gv, img):
    for part, first in ((img_0, 0), (img_n, 128), (ahead_0, 384)):

        @each(part.shape[0], 32)
        def _(span):
            img[pl.ds(pl.multiple_of(first + span.start, 32), 32)] = part[span]

    shape = gu.shape[0], txt.shape[0]
    row, col = lax.broadcasted_iota(jnp.int32, shape, 0), lax.broadcasted_iota(jnp.int32, shape, 1)
    mask = jnp.logical_and(row == col, row < 128)
    gu[...], gv[: shape[1]] = products(scalars, img[0 : shape[0]], txt[...], mask)

    @each(shape[1], 32)
    def _(span):
        there = pl.ds(pl.multiple_of(shape[1] + span.start, 32), 32)
        gv[there] = jnp.zeros((32, gv.shape[1]), F32)


def both_halves(txt):
    size = txt.shape[0] // 2

    def over(body):
        @pl.loop(0, 2)
        def _(n):
            body(n, pl.ds(pl.multiple_of(n * size, size), size))

    return over


def second_kernel(scalars, img, txt, gv_in, gu, gv):
    @each(gu.shape[0], 32)
    def _(span):
        gu[span] = jnp.zeros((32, gu.shape[1]), F32)

    @both_halves(txt)
    def _(n, here):
        part, term = products(scalars, img[...], txt[here])
        gu[...] += part
        gv[here] = term + gv_in[here]


def third_kernel(scalars, img, txt, gu_in, gu_n, gv, gu):
    @each(gu.shape[0], 32)
    def _(span):
        gu[span] = gu_in[span]

    @both_halves(txt)
    def _(n, here):
        part, gv[here] = products(scalars, img[...], txt[here])
        gu[...] += part

    gu_n[:256] = gu[...].astype(LOW)
    gu_n[256:] = jnp.zeros((16, gu_n.shape[1]), LOW)


def fourth_kernel(scalars, img, txt, gu_in, gv_in, gu, piece_0, piece_1, piece_2, piece_3, gv):
    past = gu_in.shape[0]

    @each(past, 32)
    def _(span):
        gu[span] = gu_in[span]

    @each(gu.shape[0] - past, 32)
    def _(span):
        there = pl.ds(pl.multiple_of(past + span.start, 32), 32)
        gu[there] = jnp.zeros((32, gu.shape[1]), F32)

    @both_halves(txt)
    def _(n, here):
        part, term = products(scalars, img[...], txt[here])
        gu[...] += part
        gv[...] = term + gv_in[here]
        for place, outs in enumerate(((piece_0, piece_1), (piece_2, piece_3))):

            @pl.when(n == place)
            def _():
                for m, out in enumerate(outs):

                    @each(256, 32)
                    def _(span):
                        there = pl.ds(pl.multiple_of(m * 256 + span.start, 32), 32)
                        out[span] = gv[there].astype(LOW)


def fifth_kernel(scalars, img, txt, gu_in, gv_in, gu_0, gu_up, gu_down, gu_2, au, gv, gu):
    size, past = txt.shape[0] // 2, img.shape[0] - 256
    part, term = products(scalars, img[...], txt[size:])
    gu[...] = gu_in[...] + part
    gv[size:] = term + gv_in[size:]
    part, term = products(scalars, img[past:], txt[0:size])
    gu[past:] += part
    gv[:size] = term + gv_in[:size]
    places = (gu_0, 0), (gu_up, 0), (gu_down, 0), (au, 0), (gu_2, 0), (au, 128)
    for n, (out, first) in enumerate(places):

        @each(128, 32)
        def _(span):
            rows = gu[pl.ds(pl.multiple_of(n * 128 + span.start, 32), 32)]
            out[pl.ds(pl.multiple_of(first + span.start, 32), 32)] = rows.astype(out.dtype)


def local(image_emb, text_emb, temp, bias):
    rows = image_emb.shape
    width = rows[1]
    pair, half, wide = (256, width), (512, width), (1024, width)
    (img_0,) = whole(unit_kernel, [(rows, LOW)], image_emb)
    (txt_0,) = whole(unit_kernel, [(rows, LOW)], text_emb)
    scalars = jnp.stack([0.5 * temp, 0.5 * bias])

    txt_up = to_dev(txt_0, y=-1)
    ahead_0 = to_group(img_0, -2)
    img_up = to_dev(img_0, zh=-1)
    img_down = to_dev(img_0, zh=1)
    behind_0 = to_group(txt_0, 1)
    ahead_0, txt_later = fence(ahead_0, txt_0)
    txt_down = to_dev(txt_later, y=1)
    txt_2 = to_dev(txt_later, y=2)
    txt_up, txt_down, txt_2, behind_0, img_up, img_down = fence(
        txt_up, txt_down, txt_2, behind_0, img_up, img_down
    )
    own_c, img_n, img_again = whole(
        join_kernel,
        [(half, LOW), (pair, LOW), (rows, LOW)],
        *(txt_0, txt_up, txt_down, txt_2, img_0, img_up, img_down),
    )
    own_c, img_n, behind_0, img_again = fence(own_c, img_n, behind_0, img_again)
    behind_up = to_dev(behind_0, y=-1)
    behind_down = to_dev(behind_0, y=1)
    behind_2 = to_dev(behind_0, y=2)
    ahead_n = to_group(img_n, -2)
    img_2 = to_dev(img_again, zh=2)
    gu_first, sums_c, images = whole(
        first_kernel,
        [(half, F32), (wide, F32), ((768, width), LOW)],
        *(scalars, img_again, img_n, ahead_0, own_c),
        scalars=True,
    )
    behind_up, behind_down, behind_2, ahead_n, img_2, gu_first, sums_c = fence(
        behind_up, behind_down, behind_2, ahead_n, img_2, gu_first, sums_c
    )
    txt_c = jnp.concatenate([own_c, behind_0, behind_up, behind_down, behind_2], axis=0)
    txt_s = to_dev(txt_c, core=1)
    ahead_2 = to_group(img_2, -2)
    gu_n, sums_c = whole(
        second_kernel,
        [(pair, F32), (wide, F32)],
        *(scalars, ahead_n, txt_c, sums_c),
        scalars=True,
        aliases={3: 1},
    )
    au_n, others = whole(
        third_kernel,
        [((272, width), LOW), (wide, F32)],
        *(scalars, ahead_n, txt_s, gu_n),
        scalars=True,
        scratch=[pltpu.VMEM(pair, F32)],
    )
    back_n = to_group(au_n, 2)
    images = lax.dynamic_update_slice(images, jnp.concatenate([img_2, ahead_2], axis=0), (512, 0))
    gu_all, *pieces = whole(
        fourth_kernel,
        [(images.shape, F32)] + [(pair, LOW)] * 4,
        *(scalars, images, txt_s, gu_first, others),
        scalars=True,
        scratch=[pltpu.VMEM(half, F32)],
    )
    got = [to_dev(piece, core=1) for piece in pieces]
    gu_0, gu_up, gu_down, gu_2, au, sums_c = whole(
        fifth_kernel,
        [(rows, F32)] * 4 + [(pair, LOW), (wide, F32)],
        *(scalars, images, txt_c, gu_all, sums_c),
        scalars=True,
        aliases={4: 5},
        scratch=[pltpu.VMEM(images.shape, F32)],
    )
    back_n, *got, au, sums_c = fence(back_n, *got, au, sums_c)
    sums = [(rows, F32)] + [(rows, LOW)] * 3
    sh_sum, sh_up, sh_down, sh_far = whole(
        functools.partial(text_sums_kernel, 512), sums, sums_c, *got[2:]
    )
    sum_up = (gu_up + back_n[:128].astype(F32)).astype(LOW)
    sum_down = (gu_down + back_n[128:256].astype(F32)).astype(LOW)
    sum_up, sum_down, sh_up, sh_down, au = fence(sum_up, sum_down, sh_up, sh_down, au)
    back = to_group(au, 2)
    sh_up = to_dev(sh_up, y=1)
    sum_up = to_dev(sum_up, zh=1)
    sum_down = to_dev(sum_down, zh=-1)
    sh_down = to_dev(sh_down, y=-1)
    sh_up, sh_far = fence(sh_up, sh_far)
    sh_far = to_dev(sh_far, y=2)
    own_sum, own_up, own_down, own_far = whole(
        functools.partial(text_sums_kernel, 0), sums, sums_c, *got[:2]
    )
    back_0, sum_2 = back[:128], (gu_2 + back[128:].astype(F32)).astype(LOW)
    sum_2 = to_dev(jnp.pad(sum_2, ((0, 16), (0, 0))), zh=2)
    sh_up, sum_up, sum_down, sh_down, sh_far, own_up, own_down, own_far = fence(
        sh_up, sum_up, sum_down, sh_down, sh_far, own_up, own_down, own_far
    )
    behind = (sh_sum + sh_up.astype(F32) + sh_down.astype(F32) + sh_far.astype(F32)).astype(LOW)
    behind, own_up, own_down, own_far = fence(behind, own_up, own_down, own_far)
    behind = to_group(behind, -1)
    own_up = to_dev(own_up, y=1)
    own_down = to_dev(own_down, y=-1)
    own_far = to_dev(own_far, y=2)
    (grad_image,) = whole(end_kernel, [(rows, F32)], image_emb, gu_0, sum_2, sum_up, sum_down, back_0)
    (grad_text,) = whole(end_kernel, [(rows, F32)], text_emb, own_sum, behind, own_up, own_down, own_far)
    return grad_image, grad_text


def solution(mesh):
    return jax.shard_map(
        local,
        mesh=mesh,
        in_specs=(P(("grp", "dev"), None), P(("grp", "dev"), None), P(), P()),
        out_specs=(P(("grp", "dev"), None), P(("grp", "dev"), None)),
        check_vma=False,
    )
```

```python
import functools

import jax
import jax.numpy as jnp
from jax import lax
from jax.experimental import pallas as pl
from jax.experimental.pallas import tpu as pltpu
from jax.sharding import PartitionSpec as P

X, ZL, ZH, Y, CORE = 4, 2, 4, 4, 2
GROUPS, DEVS = X * ZL, ZH * Y * CORE
F32, LOW = jnp.float32, jnp.bfloat16


def to_group(block, step):
    return lax.ppermute(block, "grp", [(i, (i + step) % GROUPS) for i in range(GROUPS)])


def to_dev(block, zh=0, y=0, core=0):
    route = []
    for i in range(DEVS):
        a, b, c = i // (Y * CORE), i // CORE % Y, i % CORE
        target = ((a + zh) % ZH * Y + (b + y) % Y) * CORE + (c + core) % CORE
        route.append((i, target))
    return lax.ppermute(block, "dev", route)


def fence(*arrays):
    return lax.optimization_barrier(arrays)


VMEM = pl.BlockSpec(memory_space=pltpu.VMEM)


def whole(kernel, outs, *operands, scalars=False, aliases=None, scratch=()):
    first = [pl.BlockSpec(memory_space=pltpu.SMEM)] if scalars else [VMEM]
    return pl.pallas_call(
        kernel,
        in_specs=first + [VMEM] * (len(operands) - 1),
        out_specs=[VMEM] * len(outs),
        out_shape=[jax.ShapeDtypeStruct(shape, kind) for shape, kind in outs],
        input_output_aliases=aliases or {},
        scratch_shapes=list(scratch),
        compiler_params=pltpu.CompilerParams(vmem_limit_bytes=28 * 1024 * 1024),
        cost_estimate=pl.CostEstimate(flops=1, bytes_accessed=1, transcendentals=0),
    )(*operands)


def inverse_of(values):
    return lax.rsqrt(jnp.sum(values * values, axis=1, keepdims=True) + 1e-06)


def each(rows, step):
    def over(body):
        @pl.loop(0, rows // step)
        def _(n):
            body(pl.ds(pl.multiple_of(n * step, step), step))

    return over


def unit_kernel(values, low):
    @each(values.shape[0], 64)
    def _(span):
        low[span] = (values[span] * inverse_of(values[span])).astype(LOW)


def end_kernel(values, own, *refs):
    *others, grad = refs

    @each(values.shape[0], 128)
    def _(span):
        sums = own[span]
        for other in others:
            sums = sums + other[span].astype(F32)
        inverse = inverse_of(values[span])
        unit = values[span] * inverse
        grad[span] = inverse * (sums - unit * jnp.sum(unit * sums, axis=1, keepdims=True))


def join_kernel(txt_0, txt_up, txt_down, txt_2, img_0, img_up, img_down, own_c, img_n, img_again):
    places = (
        *((own_c, 128 * n, part) for n, part in enumerate((txt_0, txt_up, txt_down, txt_2))),
        *((img_n, 128 * n, part) for n, part in enumerate((img_up, img_down))),
        (img_again, 0, img_0),
    )
    for out, first, part in places:

        @each(128, 64)
        def _(span):
            out[pl.ds(pl.multiple_of(first + span.start, 64), 64)] = part[span]


def text_sums_kernel(place, mine, got_0, got_1, own, up, down, far):
    for n, out in enumerate((own, up, down, far)):

        @each(128, 32)
        def _(span):
            there = pl.ds(pl.multiple_of(place + n * 128 + span.start, 32), 32)
            inside = pl.ds(pl.multiple_of(n % 2 * 128 + span.start, 32), 32)
            got = (got_0, got_1)[n // 2]
            out[span] = (mine[there] + got[inside].astype(F32)).astype(out.dtype)


def products(scalars, img, txt, mask=None):
    half_temp, half_bias = scalars[0], scalars[1]
    logits = lax.dot_general(img, txt, (((1,), (1,)), ((), ())), preferred_element_type=F32)
    slopes = half_temp * jnp.tanh(half_temp * logits + half_bias) + half_temp
    if mask is not None:
        slopes = slopes - jnp.where(mask, 2.0 * half_temp, 0.0)
    coef = slopes.astype(LOW)
    gu = jnp.dot(coef, txt, preferred_element_type=F32)
    return gu, lax.dot_general(coef, img, (((0,), (0,)), ((), ())), preferred_element_type=F32)


def first_kernel(scalars, img_0, img_n, ahead_0, txt, gu, gv, img):
    for part, first in ((img_0, 0), (img_n, 128), (ahead_0, 384)):

        @each(part.shape[0], 32)
        def _(span):
            img[pl.ds(pl.multiple_of(first + span.start, 32), 32)] = part[span]

    shape = gu.shape[0], txt.shape[0]
    row, col = lax.broadcasted_iota(jnp.int32, shape, 0), lax.broadcasted_iota(jnp.int32, shape, 1)
    mask = jnp.logical_and(row == col, row < 128)
    gu[...], gv[: shape[1]] = products(scalars, img[0 : shape[0]], txt[...], mask)

    @each(shape[1], 32)
    def _(span):
        there = pl.ds(pl.multiple_of(shape[1] + span.start, 32), 32)
        gv[there] = jnp.zeros((32, gv.shape[1]), F32)


def both_halves(txt):
    size = txt.shape[0] // 2

    def over(body):
        @pl.loop(0, 2)
        def _(n):
            body(n, pl.ds(pl.multiple_of(n * size, size), size))

    return over


def second_kernel(scalars, img, txt, gv_in, gu, gv):
    @each(gu.shape[0], 32)
    def _(span):
        gu[span] = jnp.zeros((32, gu.shape[1]), F32)

    @both_halves(txt)
    def _(n, here):
        part, term = products(scalars, img[...], txt[here])
        gu[...] += part
        gv[here] = term + gv_in[here]


def third_kernel(scalars, img, txt, gu_in, gu_n, gv, gu):
    @each(gu.shape[0], 32)
    def _(span):
        gu[span] = gu_in[span]

    @both_halves(txt)
    def _(n, here):
        part, gv[here] = products(scalars, img[...], txt[here])
        gu[...] += part

    gu_n[:256] = gu[...].astype(LOW)
    gu_n[256:] = jnp.zeros((16, gu_n.shape[1]), LOW)


def fourth_kernel(scalars, img, txt, gu_in, gv_in, gu, piece_0, piece_1, piece_2, piece_3, gv):
    past = gu_in.shape[0]

    @each(past, 32)
    def _(span):
        gu[span] = gu_in[span]

    @each(gu.shape[0] - past, 32)
    def _(span):
        there = pl.ds(pl.multiple_of(past + span.start, 32), 32)
        gu[there] = jnp.zeros((32, gu.shape[1]), F32)

    @both_halves(txt)
    def _(n, here):
        part, term = products(scalars, img[...], txt[here])
        gu[...] += part
        gv[...] = term + gv_in[here]
        for place, outs in enumerate(((piece_0, piece_1), (piece_2, piece_3))):

            @pl.when(n == place)
            def _():
                for m, out in enumerate(outs):

                    @each(256, 32)
                    def _(span):
                        there = pl.ds(pl.multiple_of(m * 256 + span.start, 32), 32)
                        out[span] = gv[there].astype(LOW)


def fifth_kernel(scalars, img, txt, gu_in, gv_in, gu_0, gu_up, gu_down, gu_2, au, gv, gu):
    size, past = txt.shape[0] // 2, img.shape[0] - 256
    part, term = products(scalars, img[...], txt[size:])
    gu[...] = gu_in[...] + part
    gv[size:] = term + gv_in[size:]
    part, term = products(scalars, img[past:], txt[0:size])
    gu[past:] += part
    gv[:size] = term + gv_in[:size]
    places = (gu_0, 0), (gu_up, 0), (gu_down, 0), (au, 0), (gu_2, 0), (au, 128)
    for n, (out, first) in enumerate(places):

        @each(128, 32)
        def _(span):
            rows = gu[pl.ds(pl.multiple_of(n * 128 + span.start, 32), 32)]
            out[pl.ds(pl.multiple_of(first + span.start, 32), 32)] = rows.astype(out.dtype)


def local(image_emb, text_emb, temp, bias):
    rows = image_emb.shape
    width = rows[1]
    pair, half, wide = (256, width), (512, width), (1024, width)
    (img_0,) = whole(unit_kernel, [(rows, LOW)], image_emb)
    (txt_0,) = whole(unit_kernel, [(rows, LOW)], text_emb)
    scalars = jnp.stack([0.5 * temp, 0.5 * bias])

    txt_up = to_dev(txt_0, y=-1)
    ahead_0 = to_group(img_0, -2)
    img_up = to_dev(img_0, zh=-1)
    img_down = to_dev(img_0, zh=1)
    behind_0 = to_group(txt_0, 1)
    ahead_0, txt_later = fence(ahead_0, txt_0)
    txt_down = to_dev(txt_later, y=1)
    txt_2 = to_dev(txt_later, y=2)
    txt_up, txt_down, txt_2, behind_0, img_up, img_down = fence(
        txt_up, txt_down, txt_2, behind_0, img_up, img_down
    )
    own_c, img_n, img_again = whole(
        join_kernel,
        [(half, LOW), (pair, LOW), (rows, LOW)],
        *(txt_0, txt_up, txt_down, txt_2, img_0, img_up, img_down),
    )
    own_c, img_n, behind_0, img_again = fence(own_c, img_n, behind_0, img_again)
    behind_up = to_dev(behind_0, y=-1)
    behind_down = to_dev(behind_0, y=1)
    behind_2 = to_dev(behind_0, y=2)
    ahead_n = to_group(img_n, -2)
    img_2 = to_dev(img_0, zh=2)
    gu_first, sums_c, images = whole(
        first_kernel,
        [(half, F32), (wide, F32), ((768, width), LOW)],
        *(scalars, img_again, img_n, ahead_0, own_c),
        scalars=True,
    )
    behind_up, behind_down, behind_2, ahead_n, img_2, gu_first, sums_c = fence(
        behind_up, behind_down, behind_2, ahead_n, img_2, gu_first, sums_c
    )
    txt_c = jnp.concatenate([own_c, behind_0, behind_up, behind_down, behind_2], axis=0)
    txt_s = to_dev(txt_c, core=1)
    ahead_2 = to_group(img_2, -2)
    gu_n, sums_c = whole(
        second_kernel,
        [(pair, F32), (wide, F32)],
        *(scalars, ahead_n, txt_c, sums_c),
        scalars=True,
        aliases={3: 1},
    )
    au_n, others = whole(
        third_kernel,
        [((272, width), LOW), (wide, F32)],
        *(scalars, ahead_n, txt_s, gu_n),
        scalars=True,
        scratch=[pltpu.VMEM(pair, F32)],
    )
    back_n = to_group(au_n, 2)
    images = lax.dynamic_update_slice(images, jnp.concatenate([img_2, ahead_2], axis=0), (512, 0))
    gu_all, *pieces = whole(
        fourth_kernel,
        [(images.shape, F32)] + [(pair, LOW)] * 4,
        *(scalars, images, txt_s, gu_first, others),
        scalars=True,
        scratch=[pltpu.VMEM(half, F32)],
    )
    got = [to_dev(piece, core=1) for piece in pieces]
    gu_0, gu_up, gu_down, gu_2, au, sums_c = whole(
        fifth_kernel,
        [(rows, F32)] * 4 + [(pair, LOW), (wide, F32)],
        *(scalars, images, txt_c, gu_all, sums_c),
        scalars=True,
        aliases={4: 5},
        scratch=[pltpu.VMEM(images.shape, F32)],
    )
    back_n, *got, au, sums_c = fence(back_n, *got, au, sums_c)
    sums = [(rows, F32)] + [(rows, LOW)] * 3
    sh_sum, sh_up, sh_down, sh_far = whole(
        functools.partial(text_sums_kernel, 512), sums, sums_c, *got[2:]
    )
    sum_up = (gu_up + back_n[:128].astype(F32)).astype(LOW)
    sum_down = (gu_down + back_n[128:256].astype(F32)).astype(LOW)
    sum_up, sum_down, sh_up, sh_down, au = fence(sum_up, sum_down, sh_up, sh_down, au)
    back = to_group(au, 2)
    sh_up = to_dev(sh_up, y=1)
    sum_up = to_dev(sum_up, zh=1)
    sum_down = to_dev(sum_down, zh=-1)
    sh_down = to_dev(sh_down, y=-1)
    sh_up, sh_far = fence(sh_up, sh_far)
    sh_far = to_dev(sh_far, y=2)
    own_sum, own_up, own_down, own_far = whole(
        functools.partial(text_sums_kernel, 0), sums, sums_c, *got[:2]
    )
    sh_up, sum_up, sum_down, sh_down, back, sh_far, own_up, own_down, own_far = fence(
        sh_up, sum_up, sum_down, sh_down, back, sh_far, own_up, own_down, own_far
    )
    back_0, sum_2 = back[:128], (gu_2 + back[128:].astype(F32)).astype(LOW)
    behind = (sh_sum + sh_up.astype(F32) + sh_down.astype(F32) + sh_far.astype(F32)).astype(LOW)
    sum_2, behind, own_up, own_down, own_far = fence(sum_2, behind, own_up, own_down, own_far)
    sum_2 = to_dev(sum_2, zh=2)
    behind = to_group(behind, -1)
    own_up = to_dev(own_up, y=1)
    own_down = to_dev(own_down, y=-1)
    own_far = to_dev(own_far, y=2)
    (grad_image,) = whole(end_kernel, [(rows, F32)], image_emb, gu_0, sum_2, sum_up, sum_down, back_0)
    (grad_text,) = whole(end_kernel, [(rows, F32)], text_emb, own_sum, behind, own_up, own_down, own_far)
    return grad_image, grad_text


def solution(mesh):
    return jax.shard_map(
        local,
        mesh=mesh,
        in_specs=(P(("grp", "dev"), None), P(("grp", "dev"), None), P(), P()),
        out_specs=(P(("grp", "dev"), None), P(("grp", "dev"), None)),
        check_vma=False,
    )
```

```python
import functools

import jax
import jax.numpy as jnp
from jax import lax
from jax.experimental import pallas as pl
from jax.experimental.pallas import tpu as pltpu
from jax.sharding import PartitionSpec as P

X, ZL, ZH, Y, CORE = 4, 2, 4, 4, 2
GROUPS, DEVS = X * ZL, ZH * Y * CORE
F32, LOW = jnp.float32, jnp.bfloat16


def to_group(block, step):
    return lax.ppermute(block, "grp", [(i, (i + step) % GROUPS) for i in range(GROUPS)])


def to_dev(block, zh=0, y=0, core=0):
    route = []
    for i in range(DEVS):
        a, b, c = i // (Y * CORE), i // CORE % Y, i % CORE
        target = ((a + zh) % ZH * Y + (b + y) % Y) * CORE + (c + core) % CORE
        route.append((i, target))
    return lax.ppermute(block, "dev", route)


def fence(*arrays):
    return lax.optimization_barrier(arrays)


VMEM = pl.BlockSpec(memory_space=pltpu.VMEM)


def whole(kernel, outs, *operands, scalars=False, aliases=None, scratch=()):
    first = [pl.BlockSpec(memory_space=pltpu.SMEM)] if scalars else [VMEM]
    return pl.pallas_call(
        kernel,
        in_specs=first + [VMEM] * (len(operands) - 1),
        out_specs=[VMEM] * len(outs),
        out_shape=[jax.ShapeDtypeStruct(shape, kind) for shape, kind in outs],
        input_output_aliases=aliases or {},
        scratch_shapes=list(scratch),
        compiler_params=pltpu.CompilerParams(vmem_limit_bytes=28 * 1024 * 1024),
        cost_estimate=pl.CostEstimate(flops=1, bytes_accessed=1, transcendentals=0),
    )(*operands)


def inverse_of(values):
    return lax.rsqrt(jnp.sum(values * values, axis=1, keepdims=True) + 1e-06)


def each(rows, step):
    def over(body):
        @pl.loop(0, rows // step)
        def _(n):
            body(pl.ds(pl.multiple_of(n * step, step), step))

    return over


def unit_kernel(values, low):
    @each(values.shape[0], 64)
    def _(span):
        low[span] = (values[span] * inverse_of(values[span])).astype(LOW)


def end_kernel(values, own, *refs):
    *others, grad = refs

    @each(values.shape[0], 128)
    def _(span):
        sums = own[span]
        for other in others:
            sums = sums + other[span].astype(F32)
        inverse = inverse_of(values[span])
        unit = values[span] * inverse
        grad[span] = inverse * (sums - unit * jnp.sum(unit * sums, axis=1, keepdims=True))


def join_kernel(txt_0, txt_up, txt_down, txt_2, img_0, img_up, img_down, own_c, img_n, img_again):
    places = (
        *((own_c, 128 * n, part) for n, part in enumerate((txt_0, txt_up, txt_down, txt_2))),
        *((img_n, 128 * n, part) for n, part in enumerate((img_up, img_down))),
        (img_again, 0, img_0),
    )
    for out, first, part in places:

        @each(128, 64)
        def _(span):
            out[pl.ds(pl.multiple_of(first + span.start, 64), 64)] = part[span]


def text_sums_kernel(place, mine, got_0, got_1, own, up, down, far):
    for n, out in enumerate((own, up, down, far)):

        @each(128, 32)
        def _(span):
            there = pl.ds(pl.multiple_of(place + n * 128 + span.start, 32), 32)
            inside = pl.ds(pl.multiple_of(n % 2 * 128 + span.start, 32), 32)
            got = (got_0, got_1)[n // 2]
            out[span] = (mine[there] + got[inside].astype(F32)).astype(out.dtype)


def products(scalars, img, txt, mask=None):
    half_temp, half_bias = scalars[0], scalars[1]
    logits = lax.dot_general(img, txt, (((1,), (1,)), ((), ())), preferred_element_type=F32)
    slopes = half_temp * jnp.tanh(half_temp * logits + half_bias) + half_temp
    if mask is not None:
        slopes = slopes - jnp.where(mask, 2.0 * half_temp, 0.0)
    coef = slopes.astype(LOW)
    gu = jnp.dot(coef, txt, preferred_element_type=F32)
    return gu, lax.dot_general(coef, img, (((0,), (0,)), ((), ())), preferred_element_type=F32)


def first_kernel(scalars, img_0, img_n, ahead_0, txt, gu, gv, img):
    for part, first in ((img_0, 0), (img_n, 128), (ahead_0, 384)):

        @each(part.shape[0], 32)
        def _(span):
            img[pl.ds(pl.multiple_of(first + span.start, 32), 32)] = part[span]

    shape = gu.shape[0] - 256, txt.shape[0]
    row, col = lax.broadcasted_iota(jnp.int32, shape, 0), lax.broadcasted_iota(jnp.int32, shape, 1)
    mask = jnp.logical_and(row == col, row < 128)
    gu[: shape[0]], gv[: shape[1]] = products(scalars, img[0 : shape[0]], txt[...], mask)

    @each(256, 32)
    def _(span):
        there = pl.ds(pl.multiple_of(shape[0] + span.start, 32), 32)
        gu[there] = jnp.zeros((32, gu.shape[1]), F32)

    @each(shape[1], 32)
    def _(span):
        there = pl.ds(pl.multiple_of(shape[1] + span.start, 32), 32)
        gv[there] = jnp.zeros((32, gv.shape[1]), F32)


def both_halves(txt, unrolled=False):
    size = txt.shape[0] // 2

    def over(body):
        if unrolled:
            for n in (0, 1):
                body(n, slice(n * size, (n + 1) * size))
            return

        @pl.loop(0, 2)
        def _(n):
            body(n, pl.ds(pl.multiple_of(n * size, size), size))

    return over


def second_kernel(scalars, img, txt, gv_in, gu, gv):
    @each(gu.shape[0], 32)
    def _(span):
        gu[span] = jnp.zeros((32, gu.shape[1]), F32)

    @both_halves(txt, unrolled=True)
    def _(n, here):
        part, term = products(scalars, img[...], txt[here])
        gu[...] += part
        gv[here] = term + gv_in[here]


def third_kernel(scalars, img, txt, gu_in, gu_n, gv, gu):
    @each(gu.shape[0], 32)
    def _(span):
        gu[span] = gu_in[span]

    @both_halves(txt, unrolled=True)
    def _(n, here):
        part, gv[here] = products(scalars, img[...], txt[here])
        gu[...] += part

    gu_n[:256] = gu[...].astype(LOW)
    gu_n[256:] = jnp.zeros((16, gu_n.shape[1]), LOW)


def fourth_kernel(scalars, img, txt, gu_in, gv_in, gu, piece_0, piece_1, piece_2, piece_3, gv):
    @both_halves(txt)
    def _(n, here):
        part, term = products(scalars, img[...], txt[here])
        gu[...] += part
        gv[...] = term + gv_in[here]
        for place, outs in enumerate(((piece_0, piece_1), (piece_2, piece_3))):

            @pl.when(n == place)
            def _():
                for m, out in enumerate(outs):

                    @each(256, 32)
                    def _(span):
                        there = pl.ds(pl.multiple_of(m * 256 + span.start, 32), 32)
                        out[span] = gv[there].astype(LOW)


def fifth_kernel(scalars, img, txt, gu_in, gv_in, gu_0, gu_up, gu_down, gu_2, au, gv):
    size, past = txt.shape[0] // 2, img.shape[0] - 256
    part, term = products(scalars, img[...], txt[size:])
    gv[size:] = term + gv_in[size:]
    last, term = products(scalars, img[past:], txt[0:size])
    gv[:size] = term + gv_in[:size]
    for first, out in ((0, gu_0), (128, gu_up), (256, gu_down)):
        out[...] = gu_in[first : first + 128] + part[first : first + 128]
    au[:128] = (gu_in[384:past] + part[384:past]).astype(LOW)
    last = last + gu_in[past:] + part[past:]
    gu_2[...] = last[:128]
    au[128:] = last[128:].astype(LOW)


def local(image_emb, text_emb, temp, bias):
    rows = image_emb.shape
    width = rows[1]
    pair, half, wide = (256, width), (512, width), (1024, width)
    (img_0,) = whole(unit_kernel, [(rows, LOW)], image_emb)
    (txt_0,) = whole(unit_kernel, [(rows, LOW)], text_emb)
    scalars = jnp.stack([0.5 * temp, 0.5 * bias])

    txt_up = to_dev(txt_0, y=-1)
    ahead_0 = to_group(img_0, -2)
    img_up = to_dev(img_0, zh=-1)
    img_down = to_dev(img_0, zh=1)
    behind_0 = to_group(txt_0, 1)
    ahead_0, txt_later = fence(ahead_0, txt_0)
    txt_down = to_dev(txt_later, y=1)
    txt_2 = to_dev(txt_later, y=2)
    txt_up, txt_down, txt_2, behind_0, img_up, img_down = fence(
        txt_up, txt_down, txt_2, behind_0, img_up, img_down
    )
    own_c, img_n, img_again = whole(
        join_kernel,
        [(half, LOW), (pair, LOW), (rows, LOW)],
        *(txt_0, txt_up, txt_down, txt_2, img_0, img_up, img_down),
    )
    own_c, img_n, behind_0, img_again = fence(own_c, img_n, behind_0, img_again)
    behind_up = to_dev(behind_0, y=-1)
    behind_down = to_dev(behind_0, y=1)
    behind_2 = to_dev(behind_0, y=2)
    ahead_n = to_group(img_n, -2)
    img_2 = to_dev(img_0, zh=2)
    gu_first, sums_c, images = whole(
        first_kernel,
        [((768, width), F32), (wide, F32), ((768, width), LOW)],
        *(scalars, img_again, img_n, ahead_0, own_c),
        scalars=True,
    )
    behind_up, behind_down, behind_2, ahead_n, img_2, gu_first, sums_c = fence(
        behind_up, behind_down, behind_2, ahead_n, img_2, gu_first, sums_c
    )
    txt_c = jnp.concatenate([own_c, behind_0, behind_up, behind_down, behind_2], axis=0)
    txt_s = to_dev(txt_c, core=1)
    ahead_2 = to_group(img_2, -2)
    gu_n, sums_c = whole(
        second_kernel,
        [(pair, F32), (wide, F32)],
        *(scalars, ahead_n, txt_c, sums_c),
        scalars=True,
        aliases={3: 1},
    )
    au_n, others = whole(
        third_kernel,
        [((272, width), LOW), (wide, F32)],
        *(scalars, ahead_n, txt_s, gu_n),
        scalars=True,
        scratch=[pltpu.VMEM(pair, F32)],
    )
    back_n = to_group(au_n, 2)
    images = lax.dynamic_update_slice(images, jnp.concatenate([img_2, ahead_2], axis=0), (512, 0))
    gu_all, *pieces = whole(
        fourth_kernel,
        [(images.shape, F32)] + [(pair, LOW)] * 4,
        *(scalars, images, txt_s, gu_first, others),
        scalars=True,
        aliases={3: 0},
        scratch=[pltpu.VMEM(half, F32)],
    )
    got = [to_dev(piece, core=1) for piece in pieces]
    gu_0, gu_up, gu_down, gu_2, au, sums_c = whole(
        fifth_kernel,
        [(rows, F32)] * 4 + [(pair, LOW), (wide, F32)],
        *(scalars, images, txt_c, gu_all, sums_c),
        scalars=True,
        aliases={4: 5},
    )
    back_n, *got, au, sums_c = fence(back_n, *got, au, sums_c)
    sums = [(rows, F32)] + [(rows, LOW)] * 3
    sh_sum, sh_up, sh_down, sh_far = whole(
        functools.partial(text_sums_kernel, 512), sums, sums_c, *got[2:]
    )
    sum_up = (gu_up + back_n[:128].astype(F32)).astype(LOW)
    sum_down = (gu_down + back_n[128:256].astype(F32)).astype(LOW)
    sum_up, sum_down, sh_up, sh_down, au = fence(sum_up, sum_down, sh_up, sh_down, au)
    back = to_group(au, 2)
    sh_up = to_dev(sh_up, y=1)
    sum_up = to_dev(sum_up, zh=1)
    sum_down = to_dev(sum_down, zh=-1)
    sh_down = to_dev(sh_down, y=-1)
    sh_up, sh_far = fence(sh_up, sh_far)
    sh_far = to_dev(sh_far, y=2)
    own_sum, own_up, own_down, own_far = whole(
        functools.partial(text_sums_kernel, 0), sums, sums_c, *got[:2]
    )
    sh_up, sum_up, sum_down, sh_down, back, sh_far, own_up, own_down, own_far = fence(
        sh_up, sum_up, sum_down, sh_down, back, sh_far, own_up, own_down, own_far
    )
    back_0, sum_2 = back[:128], (gu_2 + back[128:].astype(F32)).astype(LOW)
    behind = (sh_sum + sh_up.astype(F32) + sh_down.astype(F32) + sh_far.astype(F32)).astype(LOW)
    sum_2, behind, own_up, own_down, own_far = fence(sum_2, behind, own_up, own_down, own_far)
    sum_2 = to_dev(sum_2, zh=2)
    behind = to_group(behind, -1)
    own_up = to_dev(own_up, y=1)
    own_down = to_dev(own_down, y=-1)
    own_far = to_dev(own_far, y=2)
    (grad_image,) = whole(end_kernel, [(rows, F32)], image_emb, gu_0, sum_2, sum_up, sum_down, back_0)
    (grad_text,) = whole(end_kernel, [(rows, F32)], text_emb, own_sum, behind, own_up, own_down, own_far)
    return grad_image, grad_text


def solution(mesh):
    return jax.shard_map(
        local,
        mesh=mesh,
        in_specs=(P(("grp", "dev"), None), P(("grp", "dev"), None), P(), P()),
        out_specs=(P(("grp", "dev"), None), P(("grp", "dev"), None)),
        check_vma=False,
    )
```

```python
import functools

import jax
import jax.numpy as jnp
from jax import lax
from jax.experimental import pallas as pl
from jax.experimental.pallas import tpu as pltpu
from jax.sharding import PartitionSpec as P

X, ZL, ZH, Y, CORE = 4, 2, 4, 4, 2
GROUPS, DEVS = X * ZL, ZH * Y * CORE
F32, LOW = jnp.float32, jnp.bfloat16


def to_group(block, step):
    return lax.ppermute(block, "grp", [(i, (i + step) % GROUPS) for i in range(GROUPS)])


def to_dev(block, zh=0, y=0, core=0):
    route = []
    for i in range(DEVS):
        a, b, c = i // (Y * CORE), i // CORE % Y, i % CORE
        target = ((a + zh) % ZH * Y + (b + y) % Y) * CORE + (c + core) % CORE
        route.append((i, target))
    return lax.ppermute(block, "dev", route)


def fence(*arrays):
    return lax.optimization_barrier(arrays)


VMEM = pl.BlockSpec(memory_space=pltpu.VMEM)


def whole(kernel, outs, *operands, scalars=False, aliases=None, scratch=()):
    first = [pl.BlockSpec(memory_space=pltpu.SMEM)] if scalars else [VMEM]
    return pl.pallas_call(
        kernel,
        in_specs=first + [VMEM] * (len(operands) - 1),
        out_specs=[VMEM] * len(outs),
        out_shape=[jax.ShapeDtypeStruct(shape, kind) for shape, kind in outs],
        input_output_aliases=aliases or {},
        scratch_shapes=list(scratch),
        compiler_params=pltpu.CompilerParams(vmem_limit_bytes=28 * 1024 * 1024),
        cost_estimate=pl.CostEstimate(flops=1, bytes_accessed=1, transcendentals=0),
    )(*operands)


def inverse_of(values):
    return lax.rsqrt(jnp.sum(values * values, axis=1, keepdims=True) + 1e-06)


def each(rows, step):
    def over(body):
        @pl.loop(0, rows // step)
        def _(n):
            body(pl.ds(pl.multiple_of(n * step, step), step))

    return over


def unit_kernel(values, low):
    @each(values.shape[0], 64)
    def _(span):
        low[span] = (values[span] * inverse_of(values[span])).astype(LOW)


def end_kernel(values, own, *refs):
    *others, grad = refs

    @each(values.shape[0], 128)
    def _(span):
        sums = own[span]
        for other in others:
            sums = sums + other[span].astype(F32)
        inverse = inverse_of(values[span])
        unit = values[span] * inverse
        grad[span] = inverse * (sums - unit * jnp.sum(unit * sums, axis=1, keepdims=True))


def join_kernel(txt_0, txt_up, txt_down, txt_2, img_0, img_up, img_down, own_c, img_n, img_again):
    places = (
        *((own_c, 128 * n, part) for n, part in enumerate((txt_0, txt_up, txt_down, txt_2))),
        *((img_n, 128 * n, part) for n, part in enumerate((img_up, img_down))),
        (img_again, 0, img_0),
    )
    for out, first, part in places:

        @each(128, 64)
        def _(span):
            out[pl.ds(pl.multiple_of(first + span.start, 64), 64)] = part[span]


def text_sums_kernel(place, mine, got_0, got_1, own, up, down, far):
    for n, out in enumerate((own, up, down, far)):

        @each(128, 32)
        def _(span):
            there = pl.ds(pl.multiple_of(place + n * 128 + span.start, 32), 32)
            inside = pl.ds(pl.multiple_of(n % 2 * 128 + span.start, 32), 32)
            got = (got_0, got_1)[n // 2]
            out[span] = (mine[there] + got[inside].astype(F32)).astype(out.dtype)


def products(scalars, img, txt, mask=None):
    half_temp, half_bias = scalars[0], scalars[1]
    logits = lax.dot_general(img, txt, (((1,), (1,)), ((), ())), preferred_element_type=F32)
    slopes = half_temp * jnp.tanh(half_temp * logits + half_bias) + half_temp
    if mask is not None:
        slopes = slopes - jnp.where(mask, 2.0 * half_temp, 0.0)
    coef = slopes.astype(LOW)
    gu = jnp.dot(coef, txt, preferred_element_type=F32)
    return gu, lax.dot_general(coef, img, (((0,), (0,)), ((), ())), preferred_element_type=F32)


def first_kernel(scalars, img_0, img_n, ahead_0, txt, gu, gv, img):
    for part, first in ((img_0, 0), (img_n, 128), (ahead_0, 384)):

        @each(part.shape[0], 32)
        def _(span):
            img[pl.ds(pl.multiple_of(first + span.start, 32), 32)] = part[span]

    shape = gu.shape[0] - 256, txt.shape[0]
    row, col = lax.broadcasted_iota(jnp.int32, shape, 0), lax.broadcasted_iota(jnp.int32, shape, 1)
    mask = jnp.logical_and(row == col, row < 128)
    gu[: shape[0]], gv[: shape[1]] = products(scalars, img[0 : shape[0]], txt[...], mask)

    @each(256, 32)
    def _(span):
        there = pl.ds(pl.multiple_of(shape[0] + span.start, 32), 32)
        gu[there] = jnp.zeros((32, gu.shape[1]), F32)

    @each(shape[1], 32)
    def _(span):
        there = pl.ds(pl.multiple_of(shape[1] + span.start, 32), 32)
        gv[there] = jnp.zeros((32, gv.shape[1]), F32)


def both_halves(txt):
    size = txt.shape[0] // 2

    def over(body):
        @pl.loop(0, 2)
        def _(n):
            body(n, pl.ds(pl.multiple_of(n * size, size), size))

    return over


def second_kernel(scalars, img, txt, gv_in, gu, gv):
    size = txt.shape[0] // 2
    for n in (0, size):
        part, term = products(scalars, img[...], txt[n : n + size])
        gu[...] = part if n == 0 else gu[...] + part
        gv[n : n + size] = term + gv_in[n : n + size]


def third_kernel(scalars, img, txt, gu_in, gu_n, gv):
    size = txt.shape[0] // 2
    first, gv[:size] = products(scalars, img[...], txt[:size])
    second, gv[size:] = products(scalars, img[...], txt[size:])
    gu_n[:256] = (gu_in[...] + first + second).astype(LOW)
    gu_n[256:] = jnp.zeros((16, gu_n.shape[1]), LOW)


def fourth_kernel(scalars, img, txt, gu_in, gv_in, gu, piece_0, piece_1, piece_2, piece_3, gv):
    @both_halves(txt)
    def _(n, here):
        part, term = products(scalars, img[...], txt[here])
        gu[...] += part
        gv[...] = term + gv_in[here]
        for place, outs in enumerate(((piece_0, piece_1), (piece_2, piece_3))):

            @pl.when(n == place)
            def _():
                for m, out in enumerate(outs):

                    @each(256, 32)
                    def _(span):
                        there = pl.ds(pl.multiple_of(m * 256 + span.start, 32), 32)
                        out[span] = gv[there].astype(LOW)


def fifth_kernel(scalars, img, txt, gu_in, gv_in, gu_0, gu_up, gu_down, gu_2, au, gv):
    size, past = txt.shape[0] // 2, img.shape[0] - 256
    part, term = products(scalars, img[...], txt[size:])
    gv[size:] = term + gv_in[size:]
    last, term = products(scalars, img[past:], txt[0:size])
    gv[:size] = term + gv_in[:size]
    for first, out in ((0, gu_0), (128, gu_up), (256, gu_down)):
        out[...] = gu_in[first : first + 128] + part[first : first + 128]
    au[:128] = (gu_in[384:past] + part[384:past]).astype(LOW)
    last = last + gu_in[past:] + part[past:]
    gu_2[...] = last[:128]
    au[128:] = last[128:].astype(LOW)


def local(image_emb, text_emb, temp, bias):
    rows = image_emb.shape
    width = rows[1]
    pair, half, wide = (256, width), (512, width), (1024, width)
    (img_0,) = whole(unit_kernel, [(rows, LOW)], image_emb)
    (txt_0,) = whole(unit_kernel, [(rows, LOW)], text_emb)
    scalars = jnp.stack([0.5 * temp, 0.5 * bias])

    txt_up = to_dev(txt_0, y=-1)
    ahead_0 = to_group(img_0, -2)
    img_up = to_dev(img_0, zh=-1)
    img_down = to_dev(img_0, zh=1)
    behind_0 = to_group(txt_0, 1)
    ahead_0, txt_later = fence(ahead_0, txt_0)
    txt_down = to_dev(txt_later, y=1)
    txt_2 = to_dev(txt_later, y=2)
    txt_up, txt_down, txt_2, behind_0, img_up, img_down = fence(
        txt_up, txt_down, txt_2, behind_0, img_up, img_down
    )
    own_c, img_n, img_again = whole(
        join_kernel,
        [(half, LOW), (pair, LOW), (rows, LOW)],
        *(txt_0, txt_up, txt_down, txt_2, img_0, img_up, img_down),
    )
    own_c, img_n, behind_0, img_again = fence(own_c, img_n, behind_0, img_again)
    behind_up = to_dev(behind_0, y=-1)
    behind_down = to_dev(behind_0, y=1)
    behind_2 = to_dev(behind_0, y=2)
    ahead_n = to_group(img_n, -2)
    img_2 = to_dev(img_0, zh=2)
    gu_first, sums_c, images = whole(
        first_kernel,
        [((768, width), F32), (wide, F32), ((768, width), LOW)],
        *(scalars, img_again, img_n, ahead_0, own_c),
        scalars=True,
    )
    behind_up, behind_down, behind_2, ahead_n, img_2, gu_first, sums_c = fence(
        behind_up, behind_down, behind_2, ahead_n, img_2, gu_first, sums_c
    )
    txt_c = jnp.concatenate([own_c, behind_0, behind_up, behind_down, behind_2], axis=0)
    txt_s = to_dev(txt_c, core=1)
    ahead_2 = to_group(img_2, -2)
    gu_n, sums_c = whole(
        second_kernel,
        [(pair, F32), (wide, F32)],
        *(scalars, ahead_n, txt_c, sums_c),
        scalars=True,
        aliases={3: 1},
    )
    au_n, others = whole(
        third_kernel,
        [((272, width), LOW), (wide, F32)],
        *(scalars, ahead_n, txt_s, gu_n),
        scalars=True,
    )
    back_n = to_group(au_n, 2)
    images = lax.dynamic_update_slice(images, jnp.concatenate([img_2, ahead_2], axis=0), (512, 0))
    gu_all, *pieces = whole(
        fourth_kernel,
        [(images.shape, F32)] + [(pair, LOW)] * 4,
        *(scalars, images, txt_s, gu_first, others),
        scalars=True,
        aliases={3: 0},
        scratch=[pltpu.VMEM(half, F32)],
    )
    got = [to_dev(piece, core=1) for piece in pieces]
    gu_0, gu_up, gu_down, gu_2, au, sums_c = whole(
        fifth_kernel,
        [(rows, F32)] * 4 + [(pair, LOW), (wide, F32)],
        *(scalars, images, txt_c, gu_all, sums_c),
        scalars=True,
        aliases={4: 5},
    )
    back_n, *got, au, sums_c = fence(back_n, *got, au, sums_c)
    sums = [(rows, F32)] + [(rows, LOW)] * 3
    sh_sum, sh_up, sh_down, sh_far = whole(
        functools.partial(text_sums_kernel, 512), sums, sums_c, *got[2:]
    )
    sum_up = (gu_up + back_n[:128].astype(F32)).astype(LOW)
    sum_down = (gu_down + back_n[128:256].astype(F32)).astype(LOW)
    sum_up, sum_down, sh_up, sh_down, au = fence(sum_up, sum_down, sh_up, sh_down, au)
    back = to_group(au, 2)
    sh_up = to_dev(sh_up, y=1)
    sum_up = to_dev(sum_up, zh=1)
    sum_down = to_dev(sum_down, zh=-1)
    sh_down = to_dev(sh_down, y=-1)
    sh_up, sh_far = fence(sh_up, sh_far)
    sh_far = to_dev(sh_far, y=2)
    own_sum, own_up, own_down, own_far = whole(
        functools.partial(text_sums_kernel, 0), sums, sums_c, *got[:2]
    )
    sh_up, sum_up, sum_down, sh_down, back, sh_far, own_up, own_down, own_far = fence(
        sh_up, sum_up, sum_down, sh_down, back, sh_far, own_up, own_down, own_far
    )
    back_0, sum_2 = back[:128], (gu_2 + back[128:].astype(F32)).astype(LOW)
    behind = (sh_sum + sh_up.astype(F32) + sh_down.astype(F32) + sh_far.astype(F32)).astype(LOW)
    sum_2, behind, own_up, own_down, own_far = fence(sum_2, behind, own_up, own_down, own_far)
    sum_2 = to_dev(sum_2, zh=2)
    behind = to_group(behind, -1)
    own_up = to_dev(own_up, y=1)
    own_down = to_dev(own_down, y=-1)
    own_far = to_dev(own_far, y=2)
    (grad_image,) = whole(end_kernel, [(rows, F32)], image_emb, gu_0, sum_2, sum_up, sum_down, back_0)
    (grad_text,) = whole(end_kernel, [(rows, F32)], text_emb, own_sum, behind, own_up, own_down, own_far)
    return grad_image, grad_text


def solution(mesh):
    return jax.shard_map(
        local,
        mesh=mesh,
        in_specs=(P(("grp", "dev"), None), P(("grp", "dev"), None), P(), P()),
        out_specs=(P(("grp", "dev"), None), P(("grp", "dev"), None)),
        check_vma=False,
    )
```
